32 devices in a mesh: seq: 4 (over y, x), nbr: 8 (over z, core).
Axes of the slice: x: 2, y: 2, z: 4, core: 2. Of those that a mesh axis runs over, the one named last changes fastest.
Arguments:
- tokens: bfloat16 [2048, 4096], P(('seq', 'nbr')), may hold values from -7 to 7
- nbr_embed: bfloat16 [64, 128, 896], P('seq', 'nbr'), may hold values from -7 to 7
- neighbour_table: int32 [32, 2], P('seq'), may hold values from 0 to 63, as said below
- valid_counts: int32 [32], replicated, may hold values from 1 to 2
- dec_proj: bfloat16 [4096, 3, 4096], P(None, None, 'nbr'), may hold values from -1 to 1
- enc_query: bfloat16 [896, 4096], P(None, 'nbr'), may hold values from -2 to 2
- enc_out: bfloat16 [4096, 896], P('nbr'), may hold values from -0.09375 to 0.09375
- enc_gain: float32 [896], replicated, may hold values from 0.1 to 1.9
- nbr_proj: bfloat16 [896, 2, 4096], P(None, None, 'nbr'), may hold values from -2 to 2
- out_proj: bfloat16 [4096, 4096], P('nbr'), may hold values from -0.09375 to 0.09375
Outputs:
- cross_out: bfloat16 [2048, 4096], P(('seq', 'nbr'))
- encoded: bfloat16 [8192, 896], P(('seq', 'nbr'))
The draws below stay inside these ranges and needn't reach their ends.
Inputs may be any that keep to these rules, and one draw needn't show every extreme that they name: `neighbour_table`: for each block b of 8 groups in order, the entries of those groups are a permutation of the neighbour rows b * 16 to (b + 1) * 16 - 1.
All inputs are finite; a program needn't handle non-finite values.
Results may differ from the reference program's by a relative error of at most 0.025.
Values may be sent and summed in bfloat16 or wider, within the bound.
No kernel may reach another device: no remote copies, remote signals or barrier semaphores. Data moves between devices by JAX's collectives and lax.ppermute only.
A program may use at most 128 MiB of HBM per device.

```python
import math
import jax
import jax.numpy as jnp
from jax import lax

D = 4096
HEADS = 32
HEAD_DIM = 128
DE = 896
GROUP = 64
NLEN = 128
KN = 2
SEQ_LEN = 2048
CH_GRP = 8
NB_GRP = 16
TOKENS = 2048
GROUPS = 32
NBRS = 64


def draw_neighbour_table(key, part):
    blocks = GROUPS // CH_GRP
    block_keys = jax.random.split(jax.random.fold_in(key, 17), blocks)
    orders = jax.vmap(lambda block_key: jax.random.permutation(block_key, NB_GRP))(block_keys)
    offsets = jnp.arange(blocks, dtype=jnp.int32)[:, None] * NB_GRP
    return (orders.astype(jnp.int32) + offsets).reshape(GROUPS, KN).astype(jnp.int32)


def draw_tokens(key, part):
    values = jnp.clip(jax.random.normal(jax.random.fold_in(key, 21), (TOKENS, D), jnp.float32), -6.0, 6.0)
    return values.astype(jnp.bfloat16)


def draw_nbr_embed(key, part):
    values = jnp.clip(jax.random.normal(jax.random.fold_in(key, 31), (NBRS, NLEN, DE), jnp.float32), -6.0, 6.0)
    return values.astype(jnp.bfloat16)


def draw_dec_proj(key, part):
    values = jnp.clip(jax.random.normal(jax.random.fold_in(key, 41), (D, 3, HEADS * HEAD_DIM), jnp.float32), -4.0, 4.0) / math.sqrt(D)
    return values.astype(jnp.bfloat16)


def draw_enc_query(key, part):
    values = jnp.clip(jax.random.normal(jax.random.fold_in(key, 51), (DE, HEADS * HEAD_DIM), jnp.float32), -4.0, 4.0) / math.sqrt(DE)
    return values.astype(jnp.bfloat16)


def draw_nbr_proj(key, part):
    values = jnp.clip(jax.random.normal(jax.random.fold_in(key, 61), (DE, 2, HEADS * HEAD_DIM), jnp.float32), -4.0, 4.0) / math.sqrt(DE)
    return values.astype(jnp.bfloat16)


def plant(drawn, rng, smallest, largest):
    spot = [jax.random.randint(jax.random.fold_in(rng, axis), (), 0, length) for axis, length in enumerate(drawn.shape)]
    longest = drawn.shape.index(max(drawn.shape))
    beside = spot[:longest] + [(spot[longest] + 1) % drawn.shape[longest]] + spot[longest + 1:]
    return drawn.at[tuple(spot)].set(smallest).at[tuple(beside)].set(largest)


def steps_of(stream_key, extent, pieces, smallest, largest):
    gain, own = 1.0, jax.random.fold_in(stream_key, 6)
    for position, blocks in pieces:
        steps = jnp.exp(jax.random.uniform(jax.random.fold_in(own, position), (blocks,), jnp.float32, smallest / len(pieces), largest / len(pieces)))
        gain = gain * jnp.repeat(steps, extent[position] // blocks).reshape([-1 if axis == position else 1 for axis in range(len(extent))])
    return gain


def normal_values(stream_key, dims, deviation, limit, cuts=(), kind=jnp.bfloat16):
    entries = jax.random.normal(stream_key, dims, jnp.float32) * deviation
    if len(cuts) > 0:
        entries = steps_of(stream_key, dims, cuts, -0.22, 0.18) * entries
    return jnp.clip(entries, min=-limit, max=limit).astype(kind)


def setup_inputs(seed: int = 0) -> dict:
    streams_of = jax.random.split(jax.random.key(seed), 11)
    return {
        "tokens": draw_tokens(jax.random.fold_in(streams_of[10], 71), 0),
        "nbr_embed": draw_nbr_embed(jax.random.fold_in(streams_of[10], 71), 0),
        "neighbour_table": draw_neighbour_table(jax.random.fold_in(streams_of[10], 71), 0),
        "valid_counts": plant(jax.random.randint(streams_of[3], (GROUPS,), 1, KN + 1), jax.random.fold_in(streams_of[3], 1), 1, KN).astype(jnp.int32),
        "dec_proj": draw_dec_proj(jax.random.fold_in(streams_of[10], 71), 0),
        "enc_query": draw_enc_query(jax.random.fold_in(streams_of[10], 71), 0),
        "enc_out": normal_values(streams_of[6], (HEADS * HEAD_DIM, DE), (HEADS * HEAD_DIM) ** -0.5, 0.09375, ((0, 8),)),
        "enc_gain": jnp.clip(1.0 + 0.18 * jax.random.normal(streams_of[7], (DE,), jnp.float32), 0.1, 1.9),
        "nbr_proj": draw_nbr_proj(jax.random.fold_in(streams_of[10], 71), 0),
        "out_proj": normal_values(streams_of[9], (HEADS * HEAD_DIM, D), (HEADS * HEAD_DIM) ** -0.5, 0.09375, ((0, 8),)),
    }


def plain_softmax(scores):
    peak = lax.optimization_barrier(jnp.max(scores, axis=-1, keepdims=True))
    raised = jnp.exp(scores - peak)
    return (raised / lax.optimization_barrier(jnp.sum(raised, axis=-1, keepdims=True))).astype(jnp.bfloat16)

def masked_softmax(scores, allowed):
    live = jnp.any(allowed, axis=-1, keepdims=True)
    peak = lax.optimization_barrier(jnp.max(jnp.where(allowed, scores, -1e+30), axis=-1, keepdims=True))
    peak = jnp.where(live, peak, 0.0)
    raised = jnp.where(allowed, jnp.exp(scores - peak), 0.0)
    denominator = jnp.where(live, lax.optimization_barrier(jnp.sum(raised, axis=-1, keepdims=True)), 1.0)
    return (raised / denominator).astype(jnp.bfloat16)

def reference(tokens, nbr_embed, neighbour_table, valid_counts, dec_proj, enc_query, enc_out, enc_gain, nbr_proj, out_proj):
    all_width = HEADS * HEAD_DIM
    scale = 1.0 / HEAD_DIM ** 0.5
    projected = jnp.dot(tokens, dec_proj.reshape(D, 3 * all_width), preferred_element_type=jnp.float32).astype(jnp.bfloat16)
    projected = projected.reshape(TOKENS, 3, HEADS, HEAD_DIM)
    queries = projected[:, 0]
    cond_key = projected[:, 1].reshape(GROUPS, GROUP, HEADS, HEAD_DIM)
    cond_value = projected[:, 2].reshape(GROUPS, GROUP, HEADS, HEAD_DIM)
    row_ids = neighbour_table.reshape(-1).astype(jnp.int32)
    ordered = jnp.take(nbr_embed, row_ids, axis=0).reshape(GROUPS * KN * NLEN, DE)
    enc_queries = jnp.dot(ordered, enc_query, preferred_element_type=jnp.float32).astype(jnp.bfloat16)
    enc_queries = enc_queries.reshape(GROUPS, KN * NLEN, HEADS, HEAD_DIM)

    def enc_block(operands):
        block_query, block_key, block_value = operands
        scores = jnp.einsum('qhd,khd->hqk', block_query.astype(jnp.float32), block_key.astype(jnp.float32)) * scale
        weights = plain_softmax(scores)
        return jnp.einsum('hqk,khd->qhd', weights.astype(jnp.float32), block_value.astype(jnp.float32)).astype(jnp.bfloat16)
    enc_att = lax.map(enc_block, (enc_queries, cond_key, cond_value)).reshape(GROUPS * KN * NLEN, all_width)
    enc_sum = jnp.dot(enc_att, enc_out, preferred_element_type=jnp.float32)
    combined = ordered.astype(jnp.float32) + enc_sum
    encoded = (combined * lax.rsqrt(lax.optimization_barrier(jnp.mean(combined * combined, axis=-1, keepdims=True)) + 1e-06) * enc_gain).astype(jnp.bfloat16)
    nbr_kv = jnp.dot(encoded, nbr_proj.reshape(DE, 2 * all_width), preferred_element_type=jnp.float32).astype(jnp.bfloat16)
    nbr_kv = nbr_kv.reshape(GROUPS, KN * NLEN, 2, HEADS, HEAD_DIM)
    kv_ext = jnp.concatenate([jnp.zeros((1, KN * NLEN, 2, HEADS, HEAD_DIM), jnp.bfloat16), nbr_kv], axis=0)
    counts_ext = jnp.concatenate([jnp.zeros((1,), jnp.int32), valid_counts.astype(jnp.int32)], axis=0)
    query_pad = jnp.concatenate([jnp.zeros((1, HEADS, HEAD_DIM), jnp.bfloat16), queries, jnp.zeros((GROUP - 1, HEADS, HEAD_DIM), jnp.bfloat16)], axis=0)
    query_pad = query_pad.reshape(GROUPS + 1, GROUP, HEADS, HEAD_DIM)
    token_ids = jnp.arange((GROUPS + 1) * GROUP, dtype=jnp.int32) - 1
    active = (token_ids >= 0) & (token_ids < TOKENS) & (token_ids % SEQ_LEN >= GROUP - 1)
    active = active.reshape(GROUPS + 1, GROUP)
    key_slot = jnp.arange(KN * NLEN, dtype=jnp.int32) // NLEN

    def cca_block(operands):
        block_query, block_kv, block_count, block_active = operands
        scores = jnp.einsum('qhd,khd->hqk', block_query.astype(jnp.float32), block_kv[:, 0].astype(jnp.float32)) * scale
        allowed = block_active[None, :, None] & (key_slot < block_count)[None, None, :]
        weights = masked_softmax(scores, allowed)
        return jnp.einsum('hqk,khd->qhd', weights.astype(jnp.float32), block_kv[:, 1].astype(jnp.float32)).astype(jnp.bfloat16)
    cca_att = lax.map(cca_block, (query_pad, kv_ext, counts_ext, active))
    cca_att = cca_att.reshape((GROUPS + 1) * GROUP, all_width)[1:TOKENS + 1]
    cross_out = jnp.dot(cca_att, out_proj, preferred_element_type=jnp.float32).astype(jnp.bfloat16)
    return (cross_out, encoded)
```

```python
import functools

import jax
import jax.numpy as jnp
from jax import lax
from jax.experimental import pallas as pl
from jax.experimental.pallas import tpu as pltpu
from jax.sharding import PartitionSpec as P

HEAD_DIM = 128
GROUP = 64
NLEN = 128
SEQ_LEN = 2048
SCALE = 1.0 / HEAD_DIM**0.5
F32 = jnp.float32
BF16 = jnp.bfloat16
HBM = pl.BlockSpec(memory_space=pl.ANY)
SMEM = pl.BlockSpec(memory_space=pltpu.SMEM)
VMEM = pl.BlockSpec(memory_space=pltpu.VMEM)


def params():
    return pltpu.CompilerParams(vmem_limit_bytes=48 * 1024 * 1024)


def dot(a, b):
    return jnp.dot(a, b, preferred_element_type=F32)


def dot_t(a, b):
    return lax.dot_general(a, b, (((1,), (1,)), ((), ())), preferred_element_type=F32)


def swapped(x, nz):
    return lax.ppermute(x, "nbr", [(n, n ^ 1) for n in range(2 * nz)])


def line_gather(chip, nz):
    near, far, held = [], [], chip
    for s in range(1, nz):
        up = [(2 * z, 2 * z + 2) for z in range(s - 1, nz - 1)]
        down = [(2 * z + 1, 2 * z - 1) for z in range(1, nz - s + 1)]
        held = lax.ppermute(held, "nbr", up + down)
        near.append(held)
        arrived = [(2 * z, 2 * z + 1) for z in range(s, nz)] + [(2 * z + 1, 2 * z) for z in range(nz - s)]
        far.append(lax.ppermute(held, "nbr", arrived))
    return near, far


def line_sums(parts, other, z, core, nz):
    sign = 1 - 2 * core
    recv = None
    for s in range(1, nz):
        target = jnp.clip(z + sign * (nz - s), 0, nz - 1)
        send = lax.dynamic_index_in_dim(parts, target, 0, False).astype(F32)
        send += lax.dynamic_index_in_dim(other, target, 0, False).astype(F32)
        if recv is not None:
            send += recv.astype(F32)
        up = [(2 * t, 2 * t + 2) for t in range(0, s)]
        down = [(2 * t + 1, 2 * t - 1) for t in range(nz - s, nz)]
        recv = lax.ppermute(send.astype(BF16), "nbr", up + down)
    return recv, swapped(recv, nz)


def copies_in(pos, chip, near, far, place, sems, nz):
    z, core = pos[0], pos[1]
    todo = [(chip, z, None)]
    for s in range(1, nz):
        low = core == 0
        todo.append((near[s - 1], jnp.where(low, z - s, z + s), True))
        todo.append((far[s - 1], jnp.where(low, z + s, z - s), True))
    k = 0
    jobs = []
    for ref, j, check in todo:
        ok = None if check is None else (j >= 0) & (j < nz)
        for src, dst in place(ref, jnp.clip(j, 0, nz - 1)):
            jobs.append((ok, pltpu.make_async_copy(src, dst, sems.at[k])))
            k += 1
    return jobs


def begin(jobs):
    for ok, job in jobs:
        if ok is None:
            job.start()
        else:
            pl.when(ok)(job.start)


def finish(jobs):
    for ok, job in jobs:
        if ok is None:
            job.wait()
        else:
            pl.when(ok)(job.wait)


def proj_kernel(nz, *refs):
    pos, chip = refs[0], refs[1]
    near, far = refs[2 : nz + 1], refs[nz + 1 : 2 * nz]
    w, out, rows, sems = refs[2 * nz :]

    @pl.when(pl.program_id(0) == 0)
    def _():
        jobs = copies_in(pos, chip, near, far, lambda ref, j: [(ref, rows.at[j])], sems, nz)
        begin(jobs)
        finish(jobs)

    out[...] = dot(rows[...].reshape(-1, rows.shape[2]), w[...]).astype(BF16)


def project(pos, chip, near, far, w, nz):
    rows, depth = chip.shape
    width = w.shape[1]
    block = 256
    return pl.pallas_call(
        functools.partial(proj_kernel, nz),
        grid=(width // block,),
        in_specs=[SMEM] + [HBM] * (2 * nz - 1) + [pl.BlockSpec((depth, block), lambda i: (0, i))],
        out_specs=pl.BlockSpec((nz * rows, block), lambda i: (0, i)),
        out_shape=jax.ShapeDtypeStruct((nz * rows, width), BF16),
        scratch_shapes=[pltpu.VMEM((nz, rows, depth), BF16), pltpu.SemaphoreType.DMA((2 * nz - 1,))],
        compiler_params=params(),
        cost_estimate=pl.CostEstimate(
            flops=2 * nz * rows * depth * width, bytes_accessed=2 * depth * (width + nz * rows), transcendentals=0
        ),
        name="project",
    )(pos, chip, *near, *far, w)


def enc_kernel(nz, groups, j, *refs):
    pos, chip = refs[0], refs[1]
    near, far = refs[2 : nz + 1], refs[nz + 1 : 2 * nz]
    wq, keys, values, wo, out, own, rows, sems = refs[2 * nz :]

    def place(ref, i):
        return [(ref.at[c, j], rows.at[:, i, c]) for c in range(2)]

    jobs = copies_in(pos, chip, near, far, place, sems, nz)
    begin(jobs)
    finish(jobs)
    width = wq.shape[0]
    own[...] = rows[pos[0]].reshape(-1, width)

    def step(i, carry):
        q = dot(rows[i].reshape(-1, width), wq[...]).astype(BF16)
        here = pl.ds(pl.multiple_of((groups * i + j) * GROUP, GROUP), GROUP)
        k, v = keys[here, :], values[here, :]
        att = []
        for h in range(0, k.shape[1], HEAD_DIM):
            scores = dot_t(q[:, h : h + HEAD_DIM], k[:, h : h + HEAD_DIM]) * SCALE
            raised = jnp.exp(scores - jnp.max(scores, axis=-1, keepdims=True))
            weights = (raised / jnp.sum(raised, axis=-1, keepdims=True)).astype(BF16)
            att.append(dot(weights, v[:, h : h + HEAD_DIM]).astype(BF16))
        out[i] = dot(jnp.concatenate(att, axis=1), wo[...]).astype(BF16)
        return carry

    lax.fori_loop(0, nz, step, 0)


def encode(pos, chip, near, far, wq, projected, wo, nz, j):
    _, groups, _, part, width = chip.shape
    tokens = projected.shape[0]
    heads = wq.shape[1]
    rows = nz * 2 * part
    return pl.pallas_call(
        functools.partial(enc_kernel, nz, groups, j),
        grid=(1,),
        in_specs=[SMEM]
        + [HBM] * (2 * nz - 1)
        + [
            VMEM,
            pl.BlockSpec((tokens, heads), lambda i: (0, 1)),
            pl.BlockSpec((tokens, heads), lambda i: (0, 2)),
            VMEM,
        ],
        out_specs=[VMEM, VMEM],
        out_shape=[
            jax.ShapeDtypeStruct((nz, rows, width), BF16),
            jax.ShapeDtypeStruct((rows, width), BF16),
        ],
        scratch_shapes=[
            pltpu.VMEM((nz, nz, 2, part, width), BF16),
            pltpu.SemaphoreType.DMA((2 * (2 * nz - 1),)),
        ],
        compiler_params=params(),
        cost_estimate=pl.CostEstimate(
            flops=nz * rows * heads * (4 * width + 4 * GROUP),
            bytes_accessed=4 * nz * rows * width + 4 * heads * (width + tokens),
            transcendentals=nz * rows * heads // 2,
        ),
        name="encode",
    )(pos, chip, *near, *far, wq, projected, projected, wo)


def norm_kernel(pos, parts, other, recv, swap, raw, gain, out):
    total = parts[0].astype(F32) + other[0].astype(F32)
    total += recv[...].astype(F32) + swap[...].astype(F32)
    combined = raw[...].astype(F32) + total
    factor = lax.rsqrt(jnp.mean(combined * combined, axis=-1, keepdims=True) + 1e-06)
    out[...] = (combined * factor * gain[...]).astype(BF16)


def normed(pos, parts, other, recv, swap, raw, gain):
    shape = recv.shape
    mine = pl.BlockSpec((1,) + shape, lambda i, pos: (pos[0], 0, 0))
    flat = pl.BlockSpec(shape, lambda i, pos: (0, 0))
    return pl.pallas_call(
        norm_kernel,
        grid_spec=pltpu.PrefetchScalarGridSpec(
            num_scalar_prefetch=1,
            grid=(1,),
            in_specs=[mine, mine, flat, flat, flat, pl.BlockSpec((1, shape[1]), lambda i, pos: (0, 0))],
            out_specs=flat,
        ),
        out_shape=jax.ShapeDtypeStruct(shape, BF16),
        compiler_params=params(),
        name="normed",
    )(pos, parts, other, recv, swap, raw, gain)


def cca_kernel(nz, groups, j, *refs):
    wrap = j == groups - 1
    pos, counts, chip = refs[0], refs[1], refs[2]
    near, far = refs[3 : nz + 2], refs[nz + 2 : 2 * nz + 1]
    refs = refs[2 * nz + 1 :]
    if wrap:
        previous, refs = refs[0], refs[1:]
    queries, wkv, wo, out, rows, out_w, att, sems = refs
    load = pltpu.make_async_copy(wo, out_w, sems.at[2 * nz - 1])
    load.start()
    jobs = copies_in(pos, chip, near, far, lambda ref, i: [(ref, rows.at[i])], sems, nz)
    if wrap:
        jobs.append((None, pltpu.make_async_copy(previous, rows.at[nz], sems.at[2 * nz])))
    begin(jobs)
    finish(jobs)
    heads = queries.shape[1]
    keys = rows.shape[1]
    slot = lax.broadcasted_iota(jnp.int32, (GROUP, keys), 1) // (keys // (4 * nz)) % 2
    first = lax.broadcasted_iota(jnp.int32, (GROUP, heads), 0) == 0

    def attend(block, i):
        kv = dot(rows[i], wkv[...]).astype(BF16)
        count = counts[block]
        here = pl.ds(pl.multiple_of(block * GROUP, GROUP), GROUP)
        q = queries[here, :]
        allowed = slot < count
        parts = []
        for h in range(0, heads, HEAD_DIM):
            scores = dot_t(q[:, h : h + HEAD_DIM], kv[:, h : h + HEAD_DIM]) * SCALE
            peak = jnp.max(jnp.where(allowed, scores, -1e30), axis=-1, keepdims=True)
            raised = jnp.where(allowed, jnp.exp(jnp.where(allowed, scores - peak, 0.0)), 0.0)
            total = jnp.where(count > 0, jnp.sum(raised, axis=-1, keepdims=True), 1.0)
            weights = (raised / total).astype(BF16)
            parts.append(dot(weights, kv[:, heads + h : heads + h + HEAD_DIM]).astype(BF16))
        return jnp.concatenate(parts, axis=1)

    if wrap:
        att[0] = attend(0, nz)

        def step(i, carry):
            got = attend(groups * (i + 1), i)
            att[i] = jnp.where(first, got, att[i])
            att[jnp.minimum(i + 1, nz)] = got
            return carry
    else:

        def step(i, carry):
            att[i] = attend(groups * i + j + 1, i)
            return carry

    lax.fori_loop(0, nz, step, 0)
    load.wait()
    for i in range(nz):
        out[i] = dot(att[i], out_w[...]).astype(BF16)


def cross(pos, counts, chip, near, far, previous, queries, wkv, wo, nz, groups, j):
    keys, width = chip.shape
    heads = queries.shape[1]
    model = wo.shape[1]
    extra = [] if previous is None else [previous]
    return pl.pallas_call(
        functools.partial(cca_kernel, nz, groups, j),
        in_specs=[SMEM, SMEM] + [HBM] * (2 * nz - 1 + len(extra)) + [VMEM, VMEM, HBM],
        out_specs=VMEM,
        out_shape=jax.ShapeDtypeStruct((nz, GROUP, model), BF16),
        scratch_shapes=[
            pltpu.VMEM((nz + 1, keys, width), BF16),
            pltpu.VMEM(wo.shape, BF16),
            pltpu.VMEM((nz + 1, GROUP, heads), BF16),
            pltpu.SemaphoreType.DMA((2 * nz + 1,)),
        ],
        compiler_params=params(),
        cost_estimate=pl.CostEstimate(
            flops=2 * nz * heads * (2 * keys * width + 2 * GROUP * keys + GROUP * model),
            bytes_accessed=2 * (heads * (2 * width + model) + nz * (keys * width + GROUP * model)),
            transcendentals=nz * GROUP * keys * heads // HEAD_DIM,
        ),
        name="cross",
    )(pos, counts, chip, *near, *far, *extra, queries, wkv, wo)


def local(
    tokens,
    nbr_embed,
    neighbour_table,
    valid_counts,
    dec_proj,
    enc_query,
    enc_out,
    enc_gain,
    nbr_proj,
    out_proj,
):
    nz = lax.axis_size("nbr") // 2
    n_seq = lax.axis_size("seq")
    seq_index = lax.axis_index("seq")
    member = lax.axis_index("nbr")
    z, core = member // 2, member % 2
    pos = jnp.stack([z, core]).astype(jnp.int32)
    rows_dev, model_width = tokens.shape
    local_width = dec_proj.shape[2]
    ch_grp, slots = neighbour_table.shape
    groups = ch_grp // nz
    tok_grp = ch_grp * GROUP
    nb_grp, share, enc_width = nbr_embed.shape

    def both(own, axis=0):
        got = swapped(own, nz)
        return jnp.concatenate([jnp.where(core == 0, own, got), jnp.where(core == 0, got, own)], axis=axis)

    tok_chip = both(tokens)
    ids = neighbour_table.reshape(nz, groups, slots).transpose(1, 0, 2).reshape(-1) - seq_index * nb_grp
    ordered = jnp.take(nbr_embed, ids, axis=0, mode="clip").reshape(1, groups, nz, slots * share, enc_width)
    nbr_chip = both(ordered)
    tok_near, tok_far = line_gather(tok_chip, nz)
    nbr_near, nbr_far = line_gather(nbr_chip, nz)

    projected = project(pos, tok_chip, tok_near, tok_far, dec_proj.reshape(model_width, 3 * local_width), nz)
    queries = jnp.pad(projected[:, :local_width], ((1, GROUP - 1), (0, 0)))
    wkv = nbr_proj.reshape(enc_width, 2 * local_width)
    counts = lax.dynamic_slice_in_dim(
        jnp.concatenate([jnp.zeros((1,), jnp.int32), valid_counts]), seq_index * ch_grp, ch_grp + 1, 0
    )
    starts = (seq_index * tok_grp) % SEQ_LEN == 0
    counts = jnp.where(starts & (jnp.arange(ch_grp + 1) == 0), 0, counts)

    order = [groups - 1] + list(range(groups - 1))
    parts = {j: encode(pos, nbr_chip, nbr_near, nbr_far, enc_query, projected, enc_out, nz, j) for j in order}
    enc_own = {}
    gathered = {}
    for j in order:
        part, raw = parts[j]
        other = swapped(part, nz)
        recv, swap = line_sums(part, other, z, core, nz)
        enc_own[j] = normed(pos, part, other, recv, swap, raw, enc_gain.reshape(1, -1))
        gathered[j] = line_gather(enc_own[j], nz)

    near, far = gathered[groups - 1]
    last = enc_own[groups - 1]
    for s in range(1, nz):
        last = jnp.where(z == nz - 1 - s, jnp.where(core == 0, far[s - 1], near[s - 1]), last)
    previous = lax.ppermute(last, "seq", [(i, i + 1) for i in range(n_seq - 1)])

    sums = {}
    for j in order[1:] + order[:1]:
        part = cross(
            pos, counts, enc_own[j], *gathered[j], previous if j == groups - 1 else None,
            queries, wkv, out_proj, nz, groups, j,
        )
        other = swapped(part, nz)
        recv, swap = line_sums(part, other, z, core, nz)
        total = lax.dynamic_index_in_dim(part, z, 0, False).astype(F32)
        total += lax.dynamic_index_in_dim(other, z, 0, False).astype(F32)
        sums[j] = (total + recv.astype(F32) + swap.astype(F32)).astype(BF16)
    turn = sums[groups - 1]
    chip_out = jnp.concatenate([turn[1:]] + [sums[j] for j in range(groups - 1)] + [turn[:1]], axis=0)
    cross_out = lax.dynamic_slice_in_dim(chip_out, core * rows_dev, rows_dev, 0)

    chip_enc = jnp.stack([enc_own[j] for j in range(groups)]).reshape(groups, 2 * nz, slots, share, enc_width)
    chip_enc = chip_enc.transpose(0, 2, 1, 3, 4).reshape(-1, enc_width)
    enc_rows = chip_enc.shape[0] // 2
    encoded = lax.dynamic_slice_in_dim(chip_enc, core * enc_rows, enc_rows, 0)
    return (cross_out, encoded)


def solution(mesh):
    return jax.shard_map(
        local,
        mesh=mesh,
        in_specs=(
            P(("seq", "nbr"), None),
            P("seq", "nbr", None),
            P("seq", None),
            P(),
            P(None, None, "nbr"),
            P(None, "nbr"),
            P("nbr", None),
            P(),
            P(None, None, "nbr"),
            P("nbr", None),
        ),
        out_specs=(P(("seq", "nbr"), None), P(("seq", "nbr"), None)),
        check_vma=False,
    )
```

```python
import functools

import jax
import jax.numpy as jnp
from jax import lax
from jax.experimental import pallas as pl
from jax.experimental.pallas import tpu as pltpu
from jax.sharding import PartitionSpec as P

HEAD_DIM = 128
GROUP = 64
NLEN = 128
SEQ_LEN = 2048
SCALE = 1.0 / HEAD_DIM**0.5
F32 = jnp.float32
BF16 = jnp.bfloat16
HBM = pl.BlockSpec(memory_space=pltpu.HBM)
ANY = pl.BlockSpec(memory_space=pl.ANY)
SMEM = pl.BlockSpec(memory_space=pltpu.SMEM)
VMEM = pl.BlockSpec(memory_space=pltpu.VMEM)


def passed_along(block, axis, distance):
    devices = range(lax.axis_size(axis))
    route = [(i - distance, i) for i in devices if i - distance in devices]
    return lax.ppermute(block, axis, route)


def plain_softmax(scores):
    peak = jnp.max(scores, axis=-1, keepdims=True)
    raised = jnp.exp(scores - peak)
    return (raised / jnp.sum(raised, axis=-1, keepdims=True)).astype(jnp.bfloat16)


def masked_softmax(scores, allowed):
    live = jnp.any(allowed, axis=-1, keepdims=True)
    peak = jnp.max(jnp.where(allowed, scores, -1e30), axis=-1, keepdims=True)
    peak = jnp.where(live, peak, 0.0)
    raised = jnp.where(allowed, jnp.exp(scores - peak), 0.0)
    denominator = jnp.where(live, jnp.sum(raised, axis=-1, keepdims=True), 1.0)
    return (raised / denominator).astype(jnp.bfloat16)


def normed_rows(raw_rows, partial_sum, enc_gain):
    combined = raw_rows.astype(jnp.float32) + partial_sum
    factor = lax.rsqrt(jnp.mean(combined * combined, axis=-1, keepdims=True) + 1e-06)
    return (combined * factor * enc_gain).astype(jnp.bfloat16)


def by_heads(
    tokens,
    nbr_embed,
    neighbour_table,
    valid_counts,
    dec_proj,
    enc_query,
    enc_out,
    enc_gain,
    nbr_proj,
    out_proj,
):
    n_nbr = lax.axis_size("nbr")
    seq_index = lax.axis_index("seq")
    member = lax.axis_index("nbr")
    model_width = tokens.shape[1]
    local_width = dec_proj.shape[2]
    head_dev = local_width // HEAD_DIM
    scale = 1.0 / HEAD_DIM**0.5
    dec_flat = dec_proj.reshape(model_width, 3 * local_width)
    projected = jnp.dot(
        lax.all_gather(tokens, "nbr", axis=0, tiled=True),
        dec_flat,
        preferred_element_type=jnp.float32,
    ).astype(jnp.bfloat16)
    tok_grp = projected.shape[0]
    ch_grp = tok_grp // GROUP
    queries = projected[:, :local_width]
    cond_key = projected[:, local_width : 2 * local_width].reshape(
        ch_grp, GROUP, head_dev, HEAD_DIM
    )
    cond_value = projected[:, 2 * local_width :].reshape(ch_grp, GROUP, head_dev, HEAD_DIM)
    grp_embed = lax.all_gather(nbr_embed, "nbr", axis=1, tiled=True)
    nb_grp = grp_embed.shape[0]
    enc_width = grp_embed.shape[2]
    row_ids = neighbour_table.reshape(-1) - seq_index * nb_grp
    ordered = jnp.take(grp_embed, row_ids, axis=0).reshape(-1, enc_width)
    enc_queries = jnp.dot(ordered, enc_query, preferred_element_type=jnp.float32).astype(
        jnp.bfloat16
    )
    enc_queries = enc_queries.reshape(ch_grp, -1, head_dev, HEAD_DIM)
    enc_scores = (
        jnp.einsum("cqhd,ckhd->chqk", enc_queries, cond_key, preferred_element_type=jnp.float32)
        * scale
    )
    enc_weights = plain_softmax(enc_scores)
    enc_att = jnp.einsum(
        "chqk,ckhd->cqhd", enc_weights, cond_value, preferred_element_type=jnp.float32
    ).astype(jnp.bfloat16)
    enc_att = enc_att.reshape(-1, local_width)
    share_rows = enc_att.shape[0] // n_nbr
    summed = lax.psum(jnp.dot(enc_att, enc_out, preferred_element_type=jnp.float32), "nbr")
    encoded_all = normed_rows(ordered, summed, enc_gain)
    encoded_mine = lax.dynamic_slice_in_dim(encoded_all, member * share_rows, share_rows, 0)
    nbr_kv = jnp.dot(
        encoded_all,
        nbr_proj.reshape(enc_width, 2 * local_width),
        preferred_element_type=jnp.float32,
    ).astype(jnp.bfloat16)
    nbr_kv = nbr_kv.reshape(ch_grp, -1, 2 * local_width)
    previous = passed_along(nbr_kv[-1], "seq", 1)
    kv_ext = jnp.concatenate([previous[None], nbr_kv], axis=0)
    key_rows = kv_ext.shape[1]
    kv_ext = kv_ext.reshape(ch_grp + 1, key_rows, 2, head_dev, HEAD_DIM)
    counts_pad = jnp.concatenate([jnp.zeros((1,), jnp.int32), valid_counts], axis=0)
    counts_ext = lax.dynamic_slice_in_dim(counts_pad, seq_index * ch_grp, ch_grp + 1, 0)
    query_pad = jnp.concatenate(
        [
            jnp.zeros((1, local_width), jnp.bfloat16),
            queries,
            jnp.zeros((GROUP - 1, local_width), jnp.bfloat16),
        ],
        axis=0,
    )
    query_pad = query_pad.reshape(ch_grp + 1, GROUP, head_dev, HEAD_DIM)
    local_ids = jnp.arange((ch_grp + 1) * GROUP, dtype=jnp.int32) - 1
    global_ids = seq_index * tok_grp + local_ids
    active = (local_ids >= 0) & (local_ids < tok_grp) & (global_ids % SEQ_LEN >= GROUP - 1)
    active = active.reshape(ch_grp + 1, GROUP)
    key_slot = jnp.arange(key_rows, dtype=jnp.int32) // NLEN
    slot_live = key_slot[None, :] < counts_ext[:, None]
    allowed = active[:, None, :, None] & slot_live[:, None, None, :]
    cca_scores = (
        jnp.einsum(
            "bqhd,bkhd->bhqk", query_pad, kv_ext[:, :, 0], preferred_element_type=jnp.float32
        )
        * scale
    )
    cca_weights = masked_softmax(cca_scores, allowed)
    cca_att = jnp.einsum(
        "bhqk,bkhd->bqhd", cca_weights, kv_ext[:, :, 1], preferred_element_type=jnp.float32
    ).astype(jnp.bfloat16)
    cca_att = cca_att.reshape(-1, local_width)[1 : tok_grp + 1]
    cross_out = lax.psum_scatter(
        jnp.dot(cca_att, out_proj, preferred_element_type=jnp.float32).astype(jnp.bfloat16),
        "nbr",
        scatter_dimension=0,
        tiled=True,
    )
    return (cross_out, encoded_mine)


def params(mib):
    return pltpu.CompilerParams(vmem_limit_bytes=mib * 1024 * 1024)


def dot(a, b):
    return jnp.dot(a, b, preferred_element_type=F32)


def dot_t(a, b):
    return lax.dot_general(a, b, (((1,), (1,)), ((), ())), preferred_element_type=F32)


def swapped(x, nz):
    return lax.ppermute(x, "nbr", [(n, n ^ 1) for n in range(2 * nz)])


ENDS, MIDDLE = (0, 3), (1, 2)


def hop(x, flip, chips=(0, 1, 2, 3)):
    return lax.ppermute(x, "nbr", [(2 * z + c, 2 * (z ^ flip) + c) for z in chips for c in range(2)])


def scattered(part):
    two = part(2)
    outer = hop(two, 2, ENDS)
    three, two = part(3, two)
    passed, middle = hop(three, 1, ENDS), hop(three, 3, MIDDLE)
    one, three = part(1, three)
    one = hop(one, 1)
    inner = hop((two.astype(F32) + passed.astype(F32)).astype(BF16), 2, MIDDLE)
    own, one, outer = part(0, one, outer)
    return [own, one, outer, inner, middle]


def fetches(pos, parts, place, sems):
    inside = (pos[0] == 1) | (pos[0] == 2)
    when = [None, None, None, inside, jnp.logical_not(inside)]
    k = 0
    jobs = []
    for ref, ok, flip in zip(parts, when, (0, 1, 2, 3, 3)):
        for src, dst in place(ref, pos[0] ^ flip):
            jobs.append((ok, pltpu.make_async_copy(src, dst, sems.at[k])))
            k += 1
    return jobs


def each(jobs, act):
    for ok, job in jobs:
        if ok is None:
            act(job)
        else:
            pl.when(ok)(functools.partial(act, job))


def begin(jobs):
    each(jobs, lambda job: job.start())


def finish(jobs):
    each(jobs, lambda job: job.wait())


def proj_kernel(pos, own, other, w, mine, theirs, held, sems):
    pieces, depth, width = held.shape
    loads = [pltpu.make_async_copy(w.at[p], held.at[p], sems.at[p]) for p in range(pieces)]
    for load in loads:
        load.start()
    rows = jnp.concatenate([own[...].reshape(-1, depth), other[...].reshape(-1, depth)], axis=0)
    for p in range(pieces):
        loads[p].wait()
        got = dot(rows, held[p]).astype(BF16).reshape(2, 4, GROUP, width)
        for c, out in enumerate((mine, theirs)):
            for flip in range(4):
                out[pos[0] ^ flip, :, pl.ds(p * width, width)] = got[c, flip]


def project(pos, own, other, w):
    _, rows, depth = own.shape
    pieces, _, width = w.shape
    shape = jax.ShapeDtypeStruct((4, rows, pieces * width), BF16)
    return pl.pallas_call(
        proj_kernel,
        in_specs=[SMEM, VMEM, VMEM, HBM],
        out_specs=[VMEM, VMEM],
        out_shape=[shape, shape],
        scratch_shapes=[pltpu.VMEM(w.shape, BF16), pltpu.SemaphoreType.DMA((pieces,))],
        compiler_params=params(50),
        cost_estimate=pl.CostEstimate(
            flops=16 * rows * depth * width * pieces,
            bytes_accessed=2 * depth * (width * pieces + 8 * rows),
            transcendentals=0,
        ),
        name="project",
    )(pos, own, other, w)


def enc_kernel(flip, pos, *refs):
    parts, weights, refs = refs[:5], (refs[5:9], refs[9:13]), refs[13:]
    out, refs = refs[0], refs[1:]
    if flip == 0:
        raw, refs = refs[0], refs[1:]
    rows, att, sems = refs
    i = pos[0] ^ flip
    jobs = fetches(pos, parts, lambda ref, j: [(ref.at[c, i], rows.at[j, c]) for c in range(2)], sems)
    begin(jobs)
    finish(jobs)
    x = rows[...].reshape(out.shape)
    if flip == 0:
        raw[...] = x
    here = pl.ds(pl.multiple_of(i * GROUP, GROUP), GROUP)
    total = None
    for wq, keys, values, wo in weights:
        q = dot(x, wq[...]).astype(BF16)
        for h in range(0, wq.shape[1], HEAD_DIM):
            cols = pl.ds(h, HEAD_DIM)
            scores = dot_t(keys[here, cols], q[:, h : h + HEAD_DIM]) * SCALE
            raised = jnp.exp(scores - jnp.max(scores, axis=0, keepdims=True))
            share = (raised / jnp.sum(raised, axis=0, keepdims=True)).astype(BF16)
            att[:, cols] = lax.dot_general(
                share, values[here, cols], (((0,), (0,)), ((), ())), preferred_element_type=F32
            ).astype(BF16)
        part = dot(att[...], wo[...])
        total = part if total is None else total + part
    out[...] = total.astype(BF16)


def encode(pos, parts, flip, queries, projected, outs):
    _, _, part, width = parts[0].shape
    tokens = projected[0].shape[0]
    heads = queries[0].shape[1]
    rows = 8 * part
    kv = [pl.BlockSpec((tokens, heads), lambda i: (0, 1)), pl.BlockSpec((tokens, heads), lambda i: (0, 2))]
    shape = jax.ShapeDtypeStruct((rows, width), BF16)
    args = []
    for wq, proj, wo in zip(queries, projected, outs):
        args += [wq, proj, proj, wo]
    return pl.pallas_call(
        functools.partial(enc_kernel, flip),
        grid=(1,),
        in_specs=[SMEM] + [ANY] * 5 + ([VMEM] + kv + [VMEM]) * 2,
        out_specs=[VMEM] * (1 if flip else 2),
        out_shape=[shape] * (1 if flip else 2),
        scratch_shapes=[
            pltpu.VMEM((4, 2, part, width), BF16),
            pltpu.VMEM((rows, heads), BF16),
            pltpu.SemaphoreType.DMA((10,)),
        ],
        compiler_params=params(32),
        cost_estimate=pl.CostEstimate(
            flops=2 * rows * heads * (4 * width + 4 * GROUP),
            bytes_accessed=4 * rows * width + 8 * heads * width,
            transcendentals=rows * heads,
        ),
        name="encode",
    )(pos, *parts, *args)


def norm_kernel(nz, *refs):
    raw, gain, out = refs[nz:]
    combined = raw[...].astype(F32) + sum(r[...].astype(F32) for r in refs[:nz])
    factor = lax.rsqrt(jnp.mean(combined * combined, axis=-1, keepdims=True) + 1e-06)
    out[...] = (combined * factor * gain[...]).astype(BF16)


def normed(parts, raw, gain):
    return pl.pallas_call(
        functools.partial(norm_kernel, len(parts)),
        in_specs=[VMEM] * (len(parts) + 2),
        out_specs=VMEM,
        out_shape=jax.ShapeDtypeStruct(raw.shape, BF16),
        compiler_params=params(8),
        name="normed",
    )(*parts, raw, gain)


def attention(i, core, counts, x, wkvs, queries, out):
    keys, heads = x.shape[0], wkvs[0].shape[1] // 2
    slot = lax.broadcasted_iota(jnp.int32, (GROUP, keys), 1) // (keys // 16) % 2
    first = lax.broadcasted_iota(jnp.int32, (GROUP, 2 * heads), 0) == 0
    allowed = slot < counts[i]
    q = jnp.where(first, queries[i], queries[i + core])
    for w, wkv in enumerate(wkvs):
        kv = dot(x, wkv[...]).astype(BF16)
        for h in range(0, heads, HEAD_DIM):
            at = heads * w + h
            scores = dot_t(q[:, at : at + HEAD_DIM], kv[:, h : h + HEAD_DIM]) * SCALE
            scores = jnp.where(allowed, scores, -1e30)
            raised = jnp.where(allowed, jnp.exp(scores - jnp.max(scores, axis=-1, keepdims=True)), 0.0)
            share = (raised / jnp.sum(raised, axis=-1, keepdims=True)).astype(BF16)
            out[:, pl.ds(at, HEAD_DIM)] = dot(share, kv[:, heads + h : heads + h + HEAD_DIM]).astype(BF16)


def attend_kernel(flips, pos, counts, *refs):
    n = len(flips)
    rows, (own_kv, other_kv, queries), refs = refs[:n], refs[n : n + 3], refs[n + 3 :]
    outs = refs[-n:] if n == 1 else refs[1 : n + 1]
    for flip, x, out in zip(flips, rows, outs):
        attention(pos[0] ^ flip, pos[1], counts, x[...], (own_kv, other_kv), queries, out)
    if n > 1:
        z = pos[0]
        refs[-1][...] = jnp.where(z == 3, refs[0][...], jnp.where(z == 2, outs[0][...], outs[1][...]))


def attend(pos, counts, flips, rows, wkvs, queries, *earlier):
    keys, width = rows[0].shape
    both = wkvs[0].shape[1]
    n = len(flips)
    return pl.pallas_call(
        functools.partial(attend_kernel, flips),
        in_specs=[SMEM, SMEM] + [VMEM] * (n + 3 + len(earlier)),
        out_specs=[VMEM] * (n + len(earlier)),
        out_shape=[jax.ShapeDtypeStruct((GROUP, both), BF16)] * (n + len(earlier)),
        compiler_params=params(40),
        cost_estimate=pl.CostEstimate(
            flops=4 * n * keys * both * (width + GROUP),
            bytes_accessed=2 * (2 * width * both + n * keys * width),
            transcendentals=n * GROUP * keys * both // HEAD_DIM,
        ),
        name="attend",
    )(pos, counts, *rows, *wkvs, queries, *earlier)


def loads_of(wos, loaded, sems):
    heads, model = wos[0].shape
    pieces = sems.shape[1]
    piece = model // pieces
    return [
        [
            pltpu.make_async_copy(
                wos[w].at[:, pl.ds(p * piece, piece)], loaded.at[p, pl.ds(w * heads, heads)], sems.at[w, p]
            )
            for w in range(2)
        ]
        for p in range(pieces)
    ]


def last_kernel(pos, counts, middle, far, own_kv, other_kv, queries, *refs):
    atts, before, wos, outs, (got, held, loaded, sems) = refs[:3], refs[3], refs[4:6], refs[6:10], refs[10:]
    loads = loads_of(wos, loaded, sems)
    for load in sum(loads, []):
        load.start()
    z, core = pos[0], pos[1]
    x = jnp.where((z == 1) | (z == 2), middle[...], far[...])
    attention(z ^ 3, core, counts, x, (own_kv, other_kv), queries, got)
    held[0] = before[...]
    for flip, att in enumerate((*atts, got)):
        held[(z ^ flip) + 1] = att[...]
    first = lax.broadcasted_iota(jnp.int32, got.shape, 0) == 0
    rows = []
    for flip in range(4):
        i = (z ^ flip) + 1
        rows.append(jnp.where(first, held[i], held[i - core]))
    rows = jnp.concatenate(rows, axis=0)
    piece = loaded.shape[2]
    for p, pair in enumerate(loads):
        for load in pair:
            load.wait()
        result = dot(rows, loaded[p]).astype(BF16)
        for flip in range(4):
            outs[flip][:, pl.ds(p * piece, piece)] = result[flip * GROUP : (flip + 1) * GROUP]


def last_attend(pos, counts, middle, far, wkvs, queries, atts, before, wos):
    keys, width = middle.shape
    heads, model = wos[0].shape
    pieces = 4
    return pl.pallas_call(
        last_kernel,
        in_specs=[SMEM, SMEM] + [VMEM] * 9 + [HBM, ANY],
        out_specs=[VMEM] * 5,
        out_shape=[jax.ShapeDtypeStruct((GROUP, model), BF16)] * 4 + [jax.ShapeDtypeStruct(before.shape, BF16)],
        scratch_shapes=[
            pltpu.VMEM((5,) + before.shape, BF16),
            pltpu.VMEM((pieces, 2 * heads, model // pieces), BF16),
            pltpu.SemaphoreType.DMA((2, pieces)),
        ],
        compiler_params=params(48),
        cost_estimate=pl.CostEstimate(
            flops=16 * GROUP * heads * model + 8 * keys * heads * (width + GROUP),
            bytes_accessed=4 * heads * model + 8 * GROUP * model,
            transcendentals=2 * GROUP * keys * heads // HEAD_DIM,
        ),
        name="last_attend",
    )(pos, counts, middle, far, *wkvs, queries, *atts, before, *wos)


def late_kernel(before, own_w, other_w, out, loaded, sems):
    loads = loads_of((own_w, other_w), loaded, sems)
    for load in sum(loads, []):
        load.start()
    first = lax.broadcasted_iota(jnp.int32, before.shape, 0) == 0
    rows = jnp.where(first, 0.0, before[...].astype(F32)).astype(BF16)
    piece = loaded.shape[2]
    for p, pair in enumerate(loads):
        for load in pair:
            load.wait()
        out[:, pl.ds(p * piece, piece)] = dot(rows, loaded[p]).astype(BF16)


def late_out(before, wos):
    heads, model = wos[0].shape
    pieces = 4
    return pl.pallas_call(
        late_kernel,
        in_specs=[VMEM, HBM, ANY],
        out_specs=VMEM,
        out_shape=jax.ShapeDtypeStruct((GROUP, model), BF16),
        scratch_shapes=[
            pltpu.VMEM((pieces, 2 * heads, model // pieces), BF16),
            pltpu.SemaphoreType.DMA((2, pieces)),
        ],
        compiler_params=params(48),
        cost_estimate=pl.CostEstimate(
            flops=4 * GROUP * heads * model, bytes_accessed=4 * heads * model, transcendentals=0
        ),
        name="late_out",
    )(before, *wos)


def by_groups(
    tokens,
    nbr_embed,
    neighbour_table,
    valid_counts,
    dec_proj,
    enc_query,
    enc_out,
    enc_gain,
    nbr_proj,
    out_proj,
):
    nz = lax.axis_size("nbr") // 2
    n_seq = lax.axis_size("seq")
    seq_index = lax.axis_index("seq")
    member = lax.axis_index("nbr")
    z, core = member // 2, member % 2
    pos = jnp.stack([z, core]).astype(jnp.int32)
    width = dec_proj.shape[2]
    ch_grp, slots = neighbour_table.shape
    nb_grp, share, enc_width = nbr_embed.shape

    ids = neighbour_table.reshape(nz, 2, slots) - seq_index * nb_grp

    def picked(c):
        mine = lax.dynamic_index_in_dim(ids, c, 1, False).reshape(-1)
        return jnp.take(nbr_embed, mine, axis=0, mode="clip").reshape(nz, slots * share, enc_width)

    held = lax.optimization_barrier

    two, one = hop(tokens, 2), hop(tokens, 1)
    nbr_own = jnp.stack([picked(core), swapped(picked(1 - core), nz)])
    two, one, own, nbr_own, enc_query, enc_out, nbr_proj, out_proj = held(
        (two, one, tokens, nbr_own, enc_query, enc_out, nbr_proj, out_proj)
    )
    far, middle = hop(two, 1, MIDDLE), hop(own, 3, MIDDLE)
    nbr_two, nbr_one = hop(nbr_own, 2), hop(nbr_own, 1)
    encqs = (enc_query, swapped(enc_query, nz))
    column = jnp.stack([own, one, two, jnp.where((z == 1) | (z == 2), middle, far)])
    wkv = nbr_proj.reshape(enc_width, 2 * width)
    encos, wkvs, outps = [(w, swapped(w, nz)) for w in (enc_out, wkv, out_proj)]
    column, encos, wkvs, outps = held((column, encos, wkvs, outps))
    mine, theirs = project(pos, column, swapped(column, nz), dec_proj.transpose(1, 0, 2))
    mine, theirs, nbr_two, nbr_one, nbr_own, encqs, enc_out, nbr_proj, out_proj = held(
        (mine, theirs, nbr_two, nbr_one, nbr_own, encqs, enc_out, nbr_proj, out_proj)
    )
    nbrs = (nbr_own, nbr_one, nbr_two, hop(nbr_own, 3, MIDDLE), hop(nbr_two, 1, MIDDLE))
    projected = [p.reshape(nz * GROUP, 3 * width) for p in (mine, swapped(theirs, nz))]

    last = jnp.concatenate([p[:, :width].reshape(nz, GROUP, width)[:, GROUP - 1 :] for p in projected], axis=2)
    others = jnp.concatenate([theirs[:, :, :width], swapped(mine[:, :, :width], nz)], axis=2)
    queries = jnp.concatenate([last, others[:, : GROUP - 1]], axis=1)
    odd = range(1, 2 * nz, 2)
    back = [((q + 1) * 2 * nz + n, q * 2 * nz + n) for q in range(n_seq - 1) for n in odd]
    queries = jnp.concatenate([queries, lax.ppermute(queries[:1], ("seq", "nbr"), back)])
    counts = lax.dynamic_index_in_dim(
        lax.dynamic_slice_in_dim(valid_counts, seq_index * ch_grp, ch_grp, 0).reshape(nz, 2), core, 1, False
    )

    nbrs, queries, encos, wkvs, outps = held((nbrs, queries, encos, wkvs, outps))
    raws = []

    def part(flip, *after):
        after, here = held((after, pos))
        got = encode(here, nbrs, flip, encqs, projected, encos)
        raws.extend(got[1:])
        return [got[0], *after] if after else got[0]

    arrived = scattered(part)
    enc_own = normed(arrived, raws[0], enc_gain.reshape(1, -1))
    enc_two, enc_one = hop(enc_own, 2), hop(enc_own, 1)
    atts = list(attend(pos, counts, (0,), (enc_own,), wkvs, queries))
    enc_two, enc_mine, atts[0] = lax.optimization_barrier((enc_two, enc_own, atts[0]))
    enc_middle, enc_far = hop(enc_mine, 3, MIDDLE), hop(enc_two, 1, MIDDLE)
    *more, before = attend(pos, counts, (1, 2), (enc_one, enc_two), wkvs, queries, atts[0])
    atts += more

    def onward(x, chips):
        route = [(q * 2 * nz + 2 * i + 1, (q + 1) * 2 * nz + 2 * i + 1) for q in range(n_seq - 1) for i in chips]
        got = lax.ppermute(x, ("seq", "nbr"), route)
        return jnp.where((seq_index * ch_grp * GROUP) % SEQ_LEN == 0, 0, got).astype(BF16)

    before = onward(before, (1, 2, 3))
    *outs, last = last_attend(pos, counts, enc_middle, enc_far, wkvs, queries, atts, before, outps)
    arrived = scattered(lambda flip, *after: [outs[flip], *after] if after else outs[flip])
    arrived.append(late_out(onward(last, (0,)), outps))
    mine = sum(part.astype(F32) for part in arrived).astype(BF16)
    theirs = swapped(mine, nz)
    cross_out = jnp.concatenate([theirs[1:], mine[:1]], axis=0)

    encoded = enc_own.reshape(nz, 2, slots, share, enc_width)
    encoded = jnp.where(core == 0, encoded, encoded[:, ::-1]).transpose(2, 0, 1, 3, 4).reshape(-1, enc_width)
    return (cross_out, encoded)


def local(*args):
    tokens, table = args[0], args[2]
    chips = lax.axis_size("nbr") // 2
    if chips == 4 and table.shape[0] == 8 and tokens.shape[0] == GROUP:
        return by_groups(*args)
    return by_heads(*args)


def solution(mesh):
    return jax.shard_map(
        local,
        mesh=mesh,
        in_specs=(
            P(("seq", "nbr"), None),
            P("seq", "nbr", None),
            P("seq", None),
            P(),
            P(None, None, "nbr"),
            P(None, "nbr"),
            P("nbr", None),
            P(),
            P(None, None, "nbr"),
            P("nbr", None),
        ),
        out_specs=(P(("seq", "nbr"), None), P(("seq", "nbr"), None)),
        check_vma=False,
    )
```

```python
import functools

import jax
import jax.numpy as jnp
from jax import lax
from jax.experimental import pallas as pl
from jax.experimental.pallas import tpu as pltpu
from jax.sharding import PartitionSpec as P

HEAD_DIM = 128
GROUP = 64
NLEN = 128
SEQ_LEN = 2048
SCALE = 1.0 / HEAD_DIM**0.5
F32 = jnp.float32
BF16 = jnp.bfloat16
HBM = pl.BlockSpec(memory_space=pltpu.HBM)
ANY = pl.BlockSpec(memory_space=pl.ANY)
SMEM = pl.BlockSpec(memory_space=pltpu.SMEM)
VMEM = pl.BlockSpec(memory_space=pltpu.VMEM)


def passed_along(block, axis, distance):
    devices = range(lax.axis_size(axis))
    route = [(i - distance, i) for i in devices if i - distance in devices]
    return lax.ppermute(block, axis, route)


def plain_softmax(scores):
    peak = jnp.max(scores, axis=-1, keepdims=True)
    raised = jnp.exp(scores - peak)
    return (raised / jnp.sum(raised, axis=-1, keepdims=True)).astype(jnp.bfloat16)


def masked_softmax(scores, allowed):
    live = jnp.any(allowed, axis=-1, keepdims=True)
    peak = jnp.max(jnp.where(allowed, scores, -1e30), axis=-1, keepdims=True)
    peak = jnp.where(live, peak, 0.0)
    raised = jnp.where(allowed, jnp.exp(scores - peak), 0.0)
    denominator = jnp.where(live, jnp.sum(raised, axis=-1, keepdims=True), 1.0)
    return (raised / denominator).astype(jnp.bfloat16)


def normed_rows(raw_rows, partial_sum, enc_gain):
    combined = raw_rows.astype(jnp.float32) + partial_sum
    factor = lax.rsqrt(jnp.mean(combined * combined, axis=-1, keepdims=True) + 1e-06)
    return (combined * factor * enc_gain).astype(jnp.bfloat16)


def by_heads(
    tokens,
    nbr_embed,
    neighbour_table,
    valid_counts,
    dec_proj,
    enc_query,
    enc_out,
    enc_gain,
    nbr_proj,
    out_proj,
):
    n_nbr = lax.axis_size("nbr")
    seq_index = lax.axis_index("seq")
    member = lax.axis_index("nbr")
    model_width = tokens.shape[1]
    local_width = dec_proj.shape[2]
    head_dev = local_width // HEAD_DIM
    scale = 1.0 / HEAD_DIM**0.5
    dec_flat = dec_proj.reshape(model_width, 3 * local_width)
    projected = jnp.dot(
        lax.all_gather(tokens, "nbr", axis=0, tiled=True),
        dec_flat,
        preferred_element_type=jnp.float32,
    ).astype(jnp.bfloat16)
    tok_grp = projected.shape[0]
    ch_grp = tok_grp // GROUP
    queries = projected[:, :local_width]
    cond_key = projected[:, local_width : 2 * local_width].reshape(
        ch_grp, GROUP, head_dev, HEAD_DIM
    )
    cond_value = projected[:, 2 * local_width :].reshape(ch_grp, GROUP, head_dev, HEAD_DIM)
    grp_embed = lax.all_gather(nbr_embed, "nbr", axis=1, tiled=True)
    nb_grp = grp_embed.shape[0]
    enc_width = grp_embed.shape[2]
    row_ids = neighbour_table.reshape(-1) - seq_index * nb_grp
    ordered = jnp.take(grp_embed, row_ids, axis=0).reshape(-1, enc_width)
    enc_queries = jnp.dot(ordered, enc_query, preferred_element_type=jnp.float32).astype(
        jnp.bfloat16
    )
    enc_queries = enc_queries.reshape(ch_grp, -1, head_dev, HEAD_DIM)
    enc_scores = (
        jnp.einsum("cqhd,ckhd->chqk", enc_queries, cond_key, preferred_element_type=jnp.float32)
        * scale
    )
    enc_weights = plain_softmax(enc_scores)
    enc_att = jnp.einsum(
        "chqk,ckhd->cqhd", enc_weights, cond_value, preferred_element_type=jnp.float32
    ).astype(jnp.bfloat16)
    enc_att = enc_att.reshape(-1, local_width)
    share_rows = enc_att.shape[0] // n_nbr
    summed = lax.psum(jnp.dot(enc_att, enc_out, preferred_element_type=jnp.float32), "nbr")
    encoded_all = normed_rows(ordered, summed, enc_gain)
    encoded_mine = lax.dynamic_slice_in_dim(encoded_all, member * share_rows, share_rows, 0)
    nbr_kv = jnp.dot(
        encoded_all,
        nbr_proj.reshape(enc_width, 2 * local_width),
        preferred_element_type=jnp.float32,
    ).astype(jnp.bfloat16)
    nbr_kv = nbr_kv.reshape(ch_grp, -1, 2 * local_width)
    previous = passed_along(nbr_kv[-1], "seq", 1)
    kv_ext = jnp.concatenate([previous[None], nbr_kv], axis=0)
    key_rows = kv_ext.shape[1]
    kv_ext = kv_ext.reshape(ch_grp + 1, key_rows, 2, head_dev, HEAD_DIM)
    counts_pad = jnp.concatenate([jnp.zeros((1,), jnp.int32), valid_counts], axis=0)
    counts_ext = lax.dynamic_slice_in_dim(counts_pad, seq_index * ch_grp, ch_grp + 1, 0)
    query_pad = jnp.concatenate(
        [
            jnp.zeros((1, local_width), jnp.bfloat16),
            queries,
            jnp.zeros((GROUP - 1, local_width), jnp.bfloat16),
        ],
        axis=0,
    )
    query_pad = query_pad.reshape(ch_grp + 1, GROUP, head_dev, HEAD_DIM)
    local_ids = jnp.arange((ch_grp + 1) * GROUP, dtype=jnp.int32) - 1
    global_ids = seq_index * tok_grp + local_ids
    active = (local_ids >= 0) & (local_ids < tok_grp) & (global_ids % SEQ_LEN >= GROUP - 1)
    active = active.reshape(ch_grp + 1, GROUP)
    key_slot = jnp.arange(key_rows, dtype=jnp.int32) // NLEN
    slot_live = key_slot[None, :] < counts_ext[:, None]
    allowed = active[:, None, :, None] & slot_live[:, None, None, :]
    cca_scores = (
        jnp.einsum(
            "bqhd,bkhd->bhqk", query_pad, kv_ext[:, :, 0], preferred_element_type=jnp.float32
        )
        * scale
    )
    cca_weights = masked_softmax(cca_scores, allowed)
    cca_att = jnp.einsum(
        "bhqk,bkhd->bqhd", cca_weights, kv_ext[:, :, 1], preferred_element_type=jnp.float32
    ).astype(jnp.bfloat16)
    cca_att = cca_att.reshape(-1, local_width)[1 : tok_grp + 1]
    cross_out = lax.psum_scatter(
        jnp.dot(cca_att, out_proj, preferred_element_type=jnp.float32).astype(jnp.bfloat16),
        "nbr",
        scatter_dimension=0,
        tiled=True,
    )
    return (cross_out, encoded_mine)


def params():
    return pltpu.CompilerParams(vmem_limit_bytes=44 * 1024 * 1024)


def dot(a, b):
    return jnp.dot(a, b, preferred_element_type=F32)


def dot_t(a, b):
    return lax.dot_general(a, b, (((1,), (1,)), ((), ())), preferred_element_type=F32)


def swapped(x, nz):
    return lax.ppermute(x, "nbr", [(n, n ^ 1) for n in range(2 * nz)])


ENDS, MIDDLE = (0, 3), (1, 2)


def hop(x, flip, chips=(0, 1, 2, 3)):
    return lax.ppermute(x, "nbr", [(2 * z + c, 2 * (z ^ flip) + c) for z in chips for c in range(2)])


def scattered(part):
    two, three = part((2, 3))
    outer = hop(two, 2, ENDS)
    passed, middle = hop(three, 1, ENDS), hop(three, 3, MIDDLE)
    one, own = part((1, 0))
    one = hop(one, 1)
    inner = hop((two.astype(F32) + passed.astype(F32)).astype(BF16), 2, MIDDLE)
    return [own, one, outer, inner, middle]


def fetches(pos, parts, place, sems):
    inside = (pos[0] == 1) | (pos[0] == 2)
    when = [None, None, None, inside, jnp.logical_not(inside)]
    k = 0
    jobs = []
    for ref, ok, flip in zip(parts, when, (0, 1, 2, 3, 3)):
        for src, dst in place(ref, pos[0] ^ flip):
            jobs.append((ok, pltpu.make_async_copy(src, dst, sems.at[k])))
            k += 1
    return jobs


def each(jobs, act):
    for ok, job in jobs:
        if ok is None:
            act(job)
        else:
            pl.when(ok)(functools.partial(act, job))


def begin(jobs):
    each(jobs, lambda job: job.start())


def finish(jobs):
    each(jobs, lambda job: job.wait())


def proj_kernel(pos, own, other, w, mine, theirs, held, sems):
    pieces, depth, width = held.shape
    loads = [pltpu.make_async_copy(w.at[p], held.at[p], sems.at[p]) for p in range(pieces)]
    for load in loads:
        load.start()
    rows = jnp.concatenate([own[...].reshape(-1, depth), other[...].reshape(-1, depth)], axis=0)
    for p in range(pieces):
        loads[p].wait()
        got = dot(rows, held[p]).astype(BF16).reshape(2, 4, GROUP, width)
        for c, out in enumerate((mine, theirs)):
            for flip in range(4):
                out[pos[0] ^ flip, :, pl.ds(p * width, width)] = got[c, flip]


def project(pos, own, other, w):
    _, rows, depth = own.shape
    pieces, _, width = w.shape
    shape = jax.ShapeDtypeStruct((4, rows, pieces * width), BF16)
    return pl.pallas_call(
        proj_kernel,
        in_specs=[SMEM, VMEM, VMEM, HBM],
        out_specs=[VMEM, VMEM],
        out_shape=[shape, shape],
        scratch_shapes=[pltpu.VMEM(w.shape, BF16), pltpu.SemaphoreType.DMA((pieces,))],
        compiler_params=params(),
        cost_estimate=pl.CostEstimate(
            flops=16 * rows * depth * width * pieces,
            bytes_accessed=2 * depth * (width * pieces + 8 * rows),
            transcendentals=0,
        ),
        name="project",
    )(pos, own, other, w)


def enc_kernel(flips, pos, *refs):
    parts, weights, refs = refs[:5], (refs[5:9], refs[9:13]), refs[13:]
    n = len(flips)
    outs, (rows, att, sems) = refs[:n], refs[-3:]
    for k, flip in enumerate(flips):
        i = pos[0] ^ flip
        place = lambda ref, j: [(ref.at[c, i], rows.at[k, j, c]) for c in range(2)]
        begin(fetches(pos, parts, place, sems.at[k]))
    for k, flip in enumerate(flips):
        i = pos[0] ^ flip
        place = lambda ref, j: [(ref.at[c, i], rows.at[k, j, c]) for c in range(2)]
        finish(fetches(pos, parts, place, sems.at[k]))
    each_rows, width = outs[0].shape
    x = rows[...].reshape(n * each_rows, width)
    if flips[-1] == 0:
        refs[n][...] = x[(n - 1) * each_rows :]
    heads = weights[0][0].shape[1]
    for w, (wq, keys, values, _) in enumerate(weights):
        q = dot(x, wq[...]).astype(BF16)
        for k, flip in enumerate(flips):
            here = pl.ds(pl.multiple_of((pos[0] ^ flip) * GROUP, GROUP), GROUP)
            mine = pl.ds(k * each_rows, each_rows)
            for h in range(0, heads, HEAD_DIM):
                cols = pl.ds(h, HEAD_DIM)
                scores = dot_t(keys[here, cols], q[k * each_rows : (k + 1) * each_rows, h : h + HEAD_DIM]) * SCALE
                raised = jnp.exp(scores - jnp.max(scores, axis=0, keepdims=True))
                share = (raised / jnp.sum(raised, axis=0, keepdims=True)).astype(BF16)
                att[mine, pl.ds(w * heads + h, HEAD_DIM)] = lax.dot_general(
                    share, values[here, cols], (((0,), (0,)), ((), ())), preferred_element_type=F32
                ).astype(BF16)
    total = dot(att[:, pl.ds(0, heads)], weights[0][3][...]) + dot(att[:, pl.ds(heads, heads)], weights[1][3][...])
    for k, out in enumerate(outs):
        out[...] = total[k * each_rows : (k + 1) * each_rows].astype(BF16)


def encode(pos, parts, flips, queries, projected, outs):
    _, _, part, width = parts[0].shape
    tokens = projected[0].shape[0]
    heads = queries[0].shape[1]
    rows = 8 * part
    n = len(flips)
    kv = [pl.BlockSpec((tokens, heads), lambda i: (0, 1)), pl.BlockSpec((tokens, heads), lambda i: (0, 2))]
    args = []
    for wq, proj, wo in zip(queries, projected, outs):
        args += [wq, proj, proj, wo]
    results = n + (flips[-1] == 0)
    return pl.pallas_call(
        functools.partial(enc_kernel, flips),
        grid=(1,),
        in_specs=[SMEM] + [ANY] * 5 + ([VMEM] + kv + [VMEM]) * 2,
        out_specs=[VMEM] * results,
        out_shape=[jax.ShapeDtypeStruct((rows, width), BF16)] * results,
        scratch_shapes=[
            pltpu.VMEM((n, 4, 2, part, width), BF16),
            pltpu.VMEM((n * rows, 2 * heads), BF16),
            pltpu.SemaphoreType.DMA((n, 10)),
        ],
        compiler_params=params(),
        cost_estimate=pl.CostEstimate(
            flops=2 * n * rows * heads * (4 * width + 4 * GROUP),
            bytes_accessed=4 * n * rows * width + 8 * heads * width,
            transcendentals=n * rows * heads,
        ),
        name="encode",
    )(pos, *parts, *args)


def norm_kernel(nz, *refs):
    raw, gain, out = refs[nz:]
    combined = raw[...].astype(F32) + sum(r[...].astype(F32) for r in refs[:nz])
    factor = lax.rsqrt(jnp.mean(combined * combined, axis=-1, keepdims=True) + 1e-06)
    out[...] = (combined * factor * gain[...]).astype(BF16)


def normed(parts, raw, gain):
    return pl.pallas_call(
        functools.partial(norm_kernel, len(parts)),
        in_specs=[VMEM] * (len(parts) + 2),
        out_specs=VMEM,
        out_shape=jax.ShapeDtypeStruct(raw.shape, BF16),
        compiler_params=params(),
        name="normed",
    )(*parts, raw, gain)


def attention(i, core, counts, x, wkvs, queries, out):
    keys, heads = x.shape[0], wkvs[0].shape[1] // 2
    slot = lax.broadcasted_iota(jnp.int32, (GROUP, keys), 1) // (keys // 16) % 2
    first = lax.broadcasted_iota(jnp.int32, (GROUP, 2 * heads), 0) == 0
    allowed = slot < counts[i]
    q = jnp.where(first, queries[i], queries[i + core])
    for w, wkv in enumerate(wkvs):
        kv = dot(x, wkv[...]).astype(BF16)
        for h in range(0, heads, HEAD_DIM):
            at = heads * w + h
            scores = dot_t(q[:, at : at + HEAD_DIM], kv[:, h : h + HEAD_DIM]) * SCALE
            scores = jnp.where(allowed, scores, -1e30)
            raised = jnp.where(allowed, jnp.exp(scores - jnp.max(scores, axis=-1, keepdims=True)), 0.0)
            share = (raised / jnp.sum(raised, axis=-1, keepdims=True)).astype(BF16)
            out[:, pl.ds(at, HEAD_DIM)] = dot(share, kv[:, heads + h : heads + h + HEAD_DIM]).astype(BF16)


def attend_kernel(pos, counts, rows, own_kv, other_kv, queries, out):
    attention(pos[0], pos[1], counts, rows[...], (own_kv, other_kv), queries, out)


def attend_more_kernel(pos, counts, one, two, own_kv, other_kv, queries, first, out):
    out[0] = first[...]
    for flip, x in (1, one), (2, two):
        attention(pos[0] ^ flip, pos[1], counts, x[...], (own_kv, other_kv), queries, out.at[flip])
    z = pos[0]
    out[3] = jnp.where(z == 3, out[0], jnp.where(z == 2, out[1], out[2]))


def attend(pos, counts, rows, wkvs, queries, *earlier):
    keys, width = rows[0].shape
    both = wkvs[0].shape[1]
    n = len(rows)
    shape = (4, GROUP, both) if earlier else (GROUP, both)
    return pl.pallas_call(
        attend_more_kernel if earlier else attend_kernel,
        in_specs=[SMEM, SMEM] + [VMEM] * (n + 3 + len(earlier)),
        out_specs=VMEM,
        out_shape=jax.ShapeDtypeStruct(shape, BF16),
        compiler_params=params(),
        cost_estimate=pl.CostEstimate(
            flops=4 * n * keys * both * (width + GROUP),
            bytes_accessed=2 * (2 * width * both + n * keys * width),
            transcendentals=n * GROUP * keys * both // HEAD_DIM,
        ),
        name="attend",
    )(pos, counts, *rows, *wkvs, queries, *earlier)


def loads_of(wos, loaded, sems):
    heads, model = wos[0].shape
    pieces = sems.shape[1]
    piece = model // pieces
    return [
        [
            pltpu.make_async_copy(
                wos[w].at[:, pl.ds(p * piece, piece)], loaded.at[p, pl.ds(w * heads, heads)], sems.at[w, p]
            )
            for w in range(2)
        ]
        for p in range(pieces)
    ]


def last_kernel(pos, counts, middle, far, own_kv, other_kv, queries, *refs):
    atts, before, wos, outs, (got, held, loaded, sems) = refs[0], refs[1], refs[2:4], refs[4:8], refs[8:]
    loads = loads_of(wos, loaded, sems)
    for load in sum(loads, []):
        load.start()
    z, core = pos[0], pos[1]
    x = jnp.where((z == 1) | (z == 2), middle[...], far[...])
    attention(z ^ 3, core, counts, x, (own_kv, other_kv), queries, got)
    held[0] = before[...]
    for flip in range(4):
        held[(z ^ flip) + 1] = got[...] if flip == 3 else atts[flip]
    first = lax.broadcasted_iota(jnp.int32, got.shape, 0) == 0
    rows = []
    for flip in range(4):
        i = (z ^ flip) + 1
        rows.append(jnp.where(first, held[i], held[i - core]))
    rows = jnp.concatenate(rows, axis=0)
    piece = loaded.shape[2]
    for p, pair in enumerate(loads):
        for load in pair:
            load.wait()
        result = dot(rows, loaded[p]).astype(BF16)
        for flip in range(4):
            outs[flip][:, pl.ds(p * piece, piece)] = result[flip * GROUP : (flip + 1) * GROUP]


def last_attend(pos, counts, middle, far, wkvs, queries, atts, before, wos):
    keys, width = middle.shape
    heads, model = wos[0].shape
    pieces = 4
    return pl.pallas_call(
        last_kernel,
        in_specs=[SMEM, SMEM] + [VMEM] * 7 + [HBM, ANY],
        out_specs=[VMEM] * 5,
        out_shape=[jax.ShapeDtypeStruct((GROUP, model), BF16)] * 4 + [jax.ShapeDtypeStruct(before.shape, BF16)],
        scratch_shapes=[
            pltpu.VMEM((5,) + before.shape, BF16),
            pltpu.VMEM((pieces, 2 * heads, model // pieces), BF16),
            pltpu.SemaphoreType.DMA((2, pieces)),
        ],
        compiler_params=params(),
        cost_estimate=pl.CostEstimate(
            flops=16 * GROUP * heads * model + 8 * keys * heads * (width + GROUP),
            bytes_accessed=4 * heads * model + 8 * GROUP * model,
            transcendentals=2 * GROUP * keys * heads // HEAD_DIM,
        ),
        name="last_attend",
    )(pos, counts, middle, far, *wkvs, queries, atts, before, *wos)


def late_kernel(before, own_w, other_w, out, loaded, sems):
    loads = loads_of((own_w, other_w), loaded, sems)
    for load in sum(loads, []):
        load.start()
    first = lax.broadcasted_iota(jnp.int32, before.shape, 0) == 0
    rows = jnp.where(first, 0.0, before[...].astype(F32)).astype(BF16)
    piece = loaded.shape[2]
    for p, pair in enumerate(loads):
        for load in pair:
            load.wait()
        out[:, pl.ds(p * piece, piece)] = dot(rows, loaded[p]).astype(BF16)


def late_out(before, wos):
    heads, model = wos[0].shape
    pieces = 4
    return pl.pallas_call(
        late_kernel,
        in_specs=[VMEM, HBM, ANY],
        out_specs=VMEM,
        out_shape=jax.ShapeDtypeStruct((GROUP, model), BF16),
        scratch_shapes=[
            pltpu.VMEM((pieces, 2 * heads, model // pieces), BF16),
            pltpu.SemaphoreType.DMA((2, pieces)),
        ],
        compiler_params=params(),
        cost_estimate=pl.CostEstimate(
            flops=4 * GROUP * heads * model, bytes_accessed=4 * heads * model, transcendentals=0
        ),
        name="late_out",
    )(before, *wos)


def by_groups(
    tokens,
    nbr_embed,
    neighbour_table,
    valid_counts,
    dec_proj,
    enc_query,
    enc_out,
    enc_gain,
    nbr_proj,
    out_proj,
):
    nz = lax.axis_size("nbr") // 2
    n_seq = lax.axis_size("seq")
    seq_index = lax.axis_index("seq")
    member = lax.axis_index("nbr")
    z, core = member // 2, member % 2
    pos = jnp.stack([z, core]).astype(jnp.int32)
    width = dec_proj.shape[2]
    ch_grp, slots = neighbour_table.shape
    nb_grp, share, enc_width = nbr_embed.shape

    ids = neighbour_table.reshape(nz, 2, slots) - seq_index * nb_grp

    def picked(c):
        mine = lax.dynamic_index_in_dim(ids, c, 1, False).reshape(-1)
        return jnp.take(nbr_embed, mine, axis=0, mode="clip").reshape(nz, slots * share, enc_width)

    held = lax.optimization_barrier

    two, one = hop(tokens, 2), hop(tokens, 1)
    nbr_own = jnp.stack([picked(core), swapped(picked(1 - core), nz)])
    two, one, own, nbr_own, enc_query, enc_out, nbr_proj, out_proj = held(
        (two, one, tokens, nbr_own, enc_query, enc_out, nbr_proj, out_proj)
    )
    far, middle = hop(two, 1, MIDDLE), hop(own, 3, MIDDLE)
    wkv = nbr_proj.reshape(enc_width, 2 * width)
    encos, wkvs, outps = [(w, swapped(w, nz)) for w in (enc_out, wkv, out_proj)]
    column = jnp.stack([own, one, two, jnp.where((z == 1) | (z == 2), middle, far)])
    column, encos, wkvs, outps = held((column, encos, wkvs, outps))
    other = swapped(column, nz)
    encqs = (enc_query, swapped(enc_query, nz))
    nbr_two, nbr_one = hop(nbr_own, 2), hop(nbr_own, 1)
    mine, theirs = project(pos, column, other, dec_proj.transpose(1, 0, 2))
    mine, theirs, nbr_two, nbr_one, nbr_own, encqs = held((mine, theirs, nbr_two, nbr_one, nbr_own, encqs))
    nbrs = (nbr_own, nbr_one, nbr_two, hop(nbr_own, 3, MIDDLE), hop(nbr_two, 1, MIDDLE))
    projected = [p.reshape(nz * GROUP, 3 * width) for p in (mine, swapped(theirs, nz))]

    last = jnp.concatenate([p[:, :width].reshape(nz, GROUP, width)[:, GROUP - 1 :] for p in projected], axis=2)
    others = jnp.concatenate([theirs[:, :, :width], swapped(mine[:, :, :width], nz)], axis=2)
    queries = jnp.concatenate([last, others[:, : GROUP - 1]], axis=1)
    odd = range(1, 2 * nz, 2)
    back = [((q + 1) * 2 * nz + n, q * 2 * nz + n) for q in range(n_seq - 1) for n in odd]
    queries = jnp.concatenate([queries, lax.ppermute(queries[:1], ("seq", "nbr"), back)])
    counts = lax.dynamic_index_in_dim(
        lax.dynamic_slice_in_dim(valid_counts, seq_index * ch_grp, ch_grp, 0).reshape(nz, 2), core, 1, False
    )

    nbrs, queries = held((nbrs, queries))
    raws = []

    def part(flips):
        got = encode(pos, nbrs, flips, encqs, projected, encos)
        raws.extend(got[len(flips) :])
        return got[: len(flips)]

    arrived = scattered(part)
    enc_own = normed(arrived, raws[0], enc_gain.reshape(1, -1))
    enc_two, enc_one = hop(enc_own, 2), hop(enc_own, 1)
    first = attend(pos, counts, (enc_own,), wkvs, queries)
    enc_two, enc_mine, first = held((enc_two, enc_own, first))
    enc_middle, enc_far = hop(enc_mine, 3, MIDDLE), hop(enc_two, 1, MIDDLE)
    atts = attend(pos, counts, (enc_one, enc_two), wkvs, queries, first)

    def onward(x, chips):
        route = [(q * 2 * nz + 2 * i + 1, (q + 1) * 2 * nz + 2 * i + 1) for q in range(n_seq - 1) for i in chips]
        got = lax.ppermute(x, ("seq", "nbr"), route)
        return jnp.where((seq_index * ch_grp * GROUP) % SEQ_LEN == 0, 0, got).astype(BF16)

    before = onward(atts[3], (1, 2, 3))
    *outs, last = last_attend(pos, counts, enc_middle, enc_far, wkvs, queries, atts, before, outps)
    arrived = scattered(lambda flips: [outs[flip] for flip in flips])
    arrived.append(late_out(onward(last, (0,)), outps))
    mine = sum(part.astype(F32) for part in arrived).astype(BF16)
    theirs = swapped(mine, nz)
    cross_out = jnp.concatenate([theirs[1:], mine[:1]], axis=0)

    encoded = enc_own.reshape(nz, 2, slots, share, enc_width)
    encoded = jnp.where(core == 0, encoded, encoded[:, ::-1]).transpose(2, 0, 1, 3, 4).reshape(-1, enc_width)
    return (cross_out, encoded)


def local(*args):
    tokens, table = args[0], args[2]
    chips = lax.axis_size("nbr") // 2
    if chips == 4 and table.shape[0] == 8 and tokens.shape[0] == GROUP:
        return by_groups(*args)
    return by_heads(*args)


def solution(mesh):
    return jax.shard_map(
        local,
        mesh=mesh,
        in_specs=(
            P(("seq", "nbr"), None),
            P("seq", "nbr", None),
            P("seq", None),
            P(),
            P(None, None, "nbr"),
            P(None, "nbr"),
            P("nbr", None),
            P(),
            P(None, None, "nbr"),
            P("nbr", None),
        ),
        out_specs=(P(("seq", "nbr"), None), P(("seq", "nbr"), None)),
        check_vma=False,
    )
```

```python
import functools

import jax
import jax.numpy as jnp
from jax import lax
from jax.experimental import pallas as pl
from jax.experimental.pallas import tpu as pltpu
from jax.sharding import PartitionSpec as P

HEAD_DIM = 128
GROUP = 64
NLEN = 128
SEQ_LEN = 2048
SCALE = 1.0 / HEAD_DIM**0.5
F32 = jnp.float32
BF16 = jnp.bfloat16
HBM = pl.BlockSpec(memory_space=pltpu.HBM)
ANY = pl.BlockSpec(memory_space=pl.ANY)
SMEM = pl.BlockSpec(memory_space=pltpu.SMEM)
VMEM = pl.BlockSpec(memory_space=pltpu.VMEM)


def passed_along(block, axis, distance):
    devices = range(lax.axis_size(axis))
    route = [(i - distance, i) for i in devices if i - distance in devices]
    return lax.ppermute(block, axis, route)


def plain_softmax(scores):
    peak = jnp.max(scores, axis=-1, keepdims=True)
    raised = jnp.exp(scores - peak)
    return (raised / jnp.sum(raised, axis=-1, keepdims=True)).astype(jnp.bfloat16)


def masked_softmax(scores, allowed):
    live = jnp.any(allowed, axis=-1, keepdims=True)
    peak = jnp.max(jnp.where(allowed, scores, -1e30), axis=-1, keepdims=True)
    peak = jnp.where(live, peak, 0.0)
    raised = jnp.where(allowed, jnp.exp(scores - peak), 0.0)
    denominator = jnp.where(live, jnp.sum(raised, axis=-1, keepdims=True), 1.0)
    return (raised / denominator).astype(jnp.bfloat16)


def normed_rows(raw_rows, partial_sum, enc_gain):
    combined = raw_rows.astype(jnp.float32) + partial_sum
    factor = lax.rsqrt(jnp.mean(combined * combined, axis=-1, keepdims=True) + 1e-06)
    return (combined * factor * enc_gain).astype(jnp.bfloat16)


def by_heads(
    tokens,
    nbr_embed,
    neighbour_table,
    valid_counts,
    dec_proj,
    enc_query,
    enc_out,
    enc_gain,
    nbr_proj,
    out_proj,
):
    n_nbr = lax.axis_size("nbr")
    seq_index = lax.axis_index("seq")
    member = lax.axis_index("nbr")
    model_width = tokens.shape[1]
    local_width = dec_proj.shape[2]
    head_dev = local_width // HEAD_DIM
    scale = 1.0 / HEAD_DIM**0.5
    dec_flat = dec_proj.reshape(model_width, 3 * local_width)
    projected = jnp.dot(
        lax.all_gather(tokens, "nbr", axis=0, tiled=True),
        dec_flat,
        preferred_element_type=jnp.float32,
    ).astype(jnp.bfloat16)
    tok_grp = projected.shape[0]
    ch_grp = tok_grp // GROUP
    queries = projected[:, :local_width]
    cond_key = projected[:, local_width : 2 * local_width].reshape(
        ch_grp, GROUP, head_dev, HEAD_DIM
    )
    cond_value = projected[:, 2 * local_width :].reshape(ch_grp, GROUP, head_dev, HEAD_DIM)
    grp_embed = lax.all_gather(nbr_embed, "nbr", axis=1, tiled=True)
    nb_grp = grp_embed.shape[0]
    enc_width = grp_embed.shape[2]
    row_ids = neighbour_table.reshape(-1) - seq_index * nb_grp
    ordered = jnp.take(grp_embed, row_ids, axis=0).reshape(-1, enc_width)
    enc_queries = jnp.dot(ordered, enc_query, preferred_element_type=jnp.float32).astype(
        jnp.bfloat16
    )
    enc_queries = enc_queries.reshape(ch_grp, -1, head_dev, HEAD_DIM)
    enc_scores = (
        jnp.einsum("cqhd,ckhd->chqk", enc_queries, cond_key, preferred_element_type=jnp.float32)
        * scale
    )
    enc_weights = plain_softmax(enc_scores)
    enc_att = jnp.einsum(
        "chqk,ckhd->cqhd", enc_weights, cond_value, preferred_element_type=jnp.float32
    ).astype(jnp.bfloat16)
    enc_att = enc_att.reshape(-1, local_width)
    share_rows = enc_att.shape[0] // n_nbr
    summed = lax.psum(jnp.dot(enc_att, enc_out, preferred_element_type=jnp.float32), "nbr")
    encoded_all = normed_rows(ordered, summed, enc_gain)
    encoded_mine = lax.dynamic_slice_in_dim(encoded_all, member * share_rows, share_rows, 0)
    nbr_kv = jnp.dot(
        encoded_all,
        nbr_proj.reshape(enc_width, 2 * local_width),
        preferred_element_type=jnp.float32,
    ).astype(jnp.bfloat16)
    nbr_kv = nbr_kv.reshape(ch_grp, -1, 2 * local_width)
    previous = passed_along(nbr_kv[-1], "seq", 1)
    kv_ext = jnp.concatenate([previous[None], nbr_kv], axis=0)
    key_rows = kv_ext.shape[1]
    kv_ext = kv_ext.reshape(ch_grp + 1, key_rows, 2, head_dev, HEAD_DIM)
    counts_pad = jnp.concatenate([jnp.zeros((1,), jnp.int32), valid_counts], axis=0)
    counts_ext = lax.dynamic_slice_in_dim(counts_pad, seq_index * ch_grp, ch_grp + 1, 0)
    query_pad = jnp.concatenate(
        [
            jnp.zeros((1, local_width), jnp.bfloat16),
            queries,
            jnp.zeros((GROUP - 1, local_width), jnp.bfloat16),
        ],
        axis=0,
    )
    query_pad = query_pad.reshape(ch_grp + 1, GROUP, head_dev, HEAD_DIM)
    local_ids = jnp.arange((ch_grp + 1) * GROUP, dtype=jnp.int32) - 1
    global_ids = seq_index * tok_grp + local_ids
    active = (local_ids >= 0) & (local_ids < tok_grp) & (global_ids % SEQ_LEN >= GROUP - 1)
    active = active.reshape(ch_grp + 1, GROUP)
    key_slot = jnp.arange(key_rows, dtype=jnp.int32) // NLEN
    slot_live = key_slot[None, :] < counts_ext[:, None]
    allowed = active[:, None, :, None] & slot_live[:, None, None, :]
    cca_scores = (
        jnp.einsum(
            "bqhd,bkhd->bhqk", query_pad, kv_ext[:, :, 0], preferred_element_type=jnp.float32
        )
        * scale
    )
    cca_weights = masked_softmax(cca_scores, allowed)
    cca_att = jnp.einsum(
        "bhqk,bkhd->bqhd", cca_weights, kv_ext[:, :, 1], preferred_element_type=jnp.float32
    ).astype(jnp.bfloat16)
    cca_att = cca_att.reshape(-1, local_width)[1 : tok_grp + 1]
    cross_out = lax.psum_scatter(
        jnp.dot(cca_att, out_proj, preferred_element_type=jnp.float32).astype(jnp.bfloat16),
        "nbr",
        scatter_dimension=0,
        tiled=True,
    )
    return (cross_out, encoded_mine)


def params():
    return pltpu.CompilerParams(vmem_limit_bytes=44 * 1024 * 1024)


def dot(a, b):
    return jnp.dot(a, b, preferred_element_type=F32)


def dot_t(a, b):
    return lax.dot_general(a, b, (((1,), (1,)), ((), ())), preferred_element_type=F32)


def swapped(x, nz):
    return lax.ppermute(x, "nbr", [(n, n ^ 1) for n in range(2 * nz)])


ENDS, MIDDLE = (0, 3), (1, 2)


def hop(x, flip, chips=(0, 1, 2, 3)):
    return lax.ppermute(x, "nbr", [(2 * z + c, 2 * (z ^ flip) + c) for z in chips for c in range(2)])


def scattered(part):
    two, three = part((2, 3))
    outer = hop(two, 2, ENDS)
    passed, middle = hop(three, 1, ENDS), hop(three, 3, MIDDLE)
    one, own = part((1, 0))
    one = hop(one, 1)
    inner = hop((two.astype(F32) + passed.astype(F32)).astype(BF16), 2, MIDDLE)
    return [own, one, outer, inner, middle]


def fetches(pos, parts, place, sems):
    inside = (pos[0] == 1) | (pos[0] == 2)
    when = [None, None, None, inside, jnp.logical_not(inside)]
    k = 0
    jobs = []
    for ref, ok, flip in zip(parts, when, (0, 1, 2, 3, 3)):
        for src, dst in place(ref, pos[0] ^ flip):
            jobs.append((ok, pltpu.make_async_copy(src, dst, sems.at[k])))
            k += 1
    return jobs


def each(jobs, act):
    for ok, job in jobs:
        if ok is None:
            act(job)
        else:
            pl.when(ok)(functools.partial(act, job))


def begin(jobs):
    each(jobs, lambda job: job.start())


def finish(jobs):
    each(jobs, lambda job: job.wait())


def proj_kernel(pos, own, other, w, mine, theirs, held, sems):
    pieces, depth, width = held.shape
    loads = [pltpu.make_async_copy(w.at[p], held.at[p], sems.at[p]) for p in range(pieces)]
    for load in loads:
        load.start()
    rows = jnp.concatenate([own[...].reshape(-1, depth), other[...].reshape(-1, depth)], axis=0)
    for p in range(pieces):
        loads[p].wait()
        got = dot(rows, held[p]).astype(BF16).reshape(2, 4, GROUP, width)
        for c, out in enumerate((mine, theirs)):
            for flip in range(4):
                out[pos[0] ^ flip, :, pl.ds(p * width, width)] = got[c, flip]


def project(pos, own, other, w):
    _, rows, depth = own.shape
    pieces, _, width = w.shape
    shape = jax.ShapeDtypeStruct((4, rows, pieces * width), BF16)
    return pl.pallas_call(
        proj_kernel,
        in_specs=[SMEM, VMEM, VMEM, HBM],
        out_specs=[VMEM, VMEM],
        out_shape=[shape, shape],
        scratch_shapes=[pltpu.VMEM(w.shape, BF16), pltpu.SemaphoreType.DMA((pieces,))],
        compiler_params=params(),
        cost_estimate=pl.CostEstimate(
            flops=16 * rows * depth * width * pieces,
            bytes_accessed=2 * depth * (width * pieces + 8 * rows),
            transcendentals=0,
        ),
        name="project",
    )(pos, own, other, w)


def enc_kernel(flips, pos, *refs):
    parts, weights, refs = refs[:5], (refs[5:9], refs[9:13]), refs[13:]
    n = len(flips)
    outs, (rows, att, sems) = refs[:n], refs[-3:]
    for k, flip in enumerate(flips):
        i = pos[0] ^ flip
        place = lambda ref, j: [(ref.at[c, i], rows.at[k, j, c]) for c in range(2)]
        begin(fetches(pos, parts, place, sems.at[k]))
    for k, flip in enumerate(flips):
        i = pos[0] ^ flip
        place = lambda ref, j: [(ref.at[c, i], rows.at[k, j, c]) for c in range(2)]
        finish(fetches(pos, parts, place, sems.at[k]))
    each_rows, width = outs[0].shape
    x = rows[...].reshape(n * each_rows, width)
    if flips[-1] == 0:
        refs[n][...] = x[(n - 1) * each_rows :]
    heads = weights[0][0].shape[1]
    qs = [dot(x, wq[...]).astype(BF16) for wq, *_ in weights]
    chains = [(w, k, h) for w in range(2) for k in range(n) for h in range(0, heads, HEAD_DIM)]
    here = [pl.ds(pl.multiple_of((pos[0] ^ flip) * GROUP, GROUP), GROUP) for flip in flips]
    scores = []
    for w, k, h in chains:
        ask = qs[w][k * each_rows : (k + 1) * each_rows, h : h + HEAD_DIM]
        scores.append(dot_t(weights[w][1][here[k], pl.ds(h, HEAD_DIM)], ask)[None])
    scores = jnp.concatenate(scores, axis=0) * SCALE
    raised = jnp.exp(scores - jnp.max(scores, axis=1, keepdims=True))
    share = (raised / jnp.sum(raised, axis=1, keepdims=True)).astype(BF16)
    for c, (w, k, h) in enumerate(chains):
        att[pl.ds(k * each_rows, each_rows), pl.ds(w * heads + h, HEAD_DIM)] = lax.dot_general(
            share[c],
            weights[w][2][here[k], pl.ds(h, HEAD_DIM)],
            (((0,), (0,)), ((), ())),
            preferred_element_type=F32,
        ).astype(BF16)
    total = dot(att[:, pl.ds(0, heads)], weights[0][3][...]) + dot(att[:, pl.ds(heads, heads)], weights[1][3][...])
    for k, out in enumerate(outs):
        out[...] = total[k * each_rows : (k + 1) * each_rows].astype(BF16)


def encode(pos, parts, flips, queries, projected, outs):
    _, _, part, width = parts[0].shape
    tokens = projected[0].shape[0]
    heads = queries[0].shape[1]
    rows = 8 * part
    n = len(flips)
    kv = [pl.BlockSpec((tokens, heads), lambda i: (0, 1)), pl.BlockSpec((tokens, heads), lambda i: (0, 2))]
    args = []
    for wq, proj, wo in zip(queries, projected, outs):
        args += [wq, proj, proj, wo]
    results = n + (flips[-1] == 0)
    return pl.pallas_call(
        functools.partial(enc_kernel, flips),
        grid=(1,),
        in_specs=[SMEM] + [ANY] * 5 + ([VMEM] + kv + [VMEM]) * 2,
        out_specs=[VMEM] * results,
        out_shape=[jax.ShapeDtypeStruct((rows, width), BF16)] * results,
        scratch_shapes=[
            pltpu.VMEM((n, 4, 2, part, width), BF16),
            pltpu.VMEM((n * rows, 2 * heads), BF16),
            pltpu.SemaphoreType.DMA((n, 10)),
        ],
        compiler_params=params(),
        cost_estimate=pl.CostEstimate(
            flops=2 * n * rows * heads * (4 * width + 4 * GROUP),
            bytes_accessed=4 * n * rows * width + 8 * heads * width,
            transcendentals=n * rows * heads,
        ),
        name="encode",
    )(pos, *parts, *args)


def norm_kernel(nz, *refs):
    raw, gain, out = refs[nz:]
    combined = raw[...].astype(F32) + sum(r[...].astype(F32) for r in refs[:nz])
    factor = lax.rsqrt(jnp.mean(combined * combined, axis=-1, keepdims=True) + 1e-06)
    out[...] = (combined * factor * gain[...]).astype(BF16)


def normed(parts, raw, gain):
    return pl.pallas_call(
        functools.partial(norm_kernel, len(parts)),
        in_specs=[VMEM] * (len(parts) + 2),
        out_specs=VMEM,
        out_shape=jax.ShapeDtypeStruct(raw.shape, BF16),
        compiler_params=params(),
        name="normed",
    )(*parts, raw, gain)


def attention(i, core, counts, x, wkvs, queries, out):
    keys, heads = x.shape[0], wkvs[0].shape[1] // 2
    slot = lax.broadcasted_iota(jnp.int32, (GROUP, keys), 1) // (keys // 16) % 2
    first = lax.broadcasted_iota(jnp.int32, (GROUP, 2 * heads), 0) == 0
    allowed = slot < counts[i]
    q = jnp.where(first, queries[i], queries[i + core])
    kvs = [dot(x, wkv[...]).astype(BF16) for wkv in wkvs]
    each_head = [(w, h) for w in range(2) for h in range(0, heads, HEAD_DIM)]
    scores = [
        dot_t(q[:, heads * w + h : heads * w + h + HEAD_DIM], kvs[w][:, h : h + HEAD_DIM]) for w, h in each_head
    ]
    scores = jnp.concatenate(scores, axis=0) * SCALE
    allowed = jnp.concatenate([allowed] * len(each_head), axis=0)
    scores = jnp.where(allowed, scores, -1e30)
    raised = jnp.where(allowed, jnp.exp(scores - jnp.max(scores, axis=-1, keepdims=True)), 0.0)
    share = (raised / jnp.sum(raised, axis=-1, keepdims=True)).astype(BF16)
    for k, (w, h) in enumerate(each_head):
        value = kvs[w][:, heads + h : heads + h + HEAD_DIM]
        out[:, pl.ds(heads * w + h, HEAD_DIM)] = dot(share[k * GROUP : (k + 1) * GROUP], value).astype(BF16)


def attend_kernel(pos, counts, rows, own_kv, other_kv, queries, out):
    attention(pos[0], pos[1], counts, rows[...], (own_kv, other_kv), queries, out)


def attend_more_kernel(pos, counts, one, two, own_kv, other_kv, queries, first, out):
    out[0] = first[...]
    for flip, x in (1, one), (2, two):
        attention(pos[0] ^ flip, pos[1], counts, x[...], (own_kv, other_kv), queries, out.at[flip])
    z = pos[0]
    out[3] = jnp.where(z == 3, out[0], jnp.where(z == 2, out[1], out[2]))


def attend(pos, counts, rows, wkvs, queries, *earlier):
    keys, width = rows[0].shape
    both = wkvs[0].shape[1]
    n = len(rows)
    shape = (4, GROUP, both) if earlier else (GROUP, both)
    return pl.pallas_call(
        attend_more_kernel if earlier else attend_kernel,
        in_specs=[SMEM, SMEM] + [VMEM] * (n + 3 + len(earlier)),
        out_specs=VMEM,
        out_shape=jax.ShapeDtypeStruct(shape, BF16),
        compiler_params=params(),
        cost_estimate=pl.CostEstimate(
            flops=4 * n * keys * both * (width + GROUP),
            bytes_accessed=2 * (2 * width * both + n * keys * width),
            transcendentals=n * GROUP * keys * both // HEAD_DIM,
        ),
        name="attend",
    )(pos, counts, *rows, *wkvs, queries, *earlier)


def loads_of(wos, loaded, sems):
    heads, model = wos[0].shape
    pieces = sems.shape[1]
    piece = model // pieces
    return [
        [
            pltpu.make_async_copy(
                wos[w].at[:, pl.ds(p * piece, piece)], loaded.at[p, pl.ds(w * heads, heads)], sems.at[w, p]
            )
            for w in range(2)
        ]
        for p in range(pieces)
    ]


def last_kernel(pos, counts, middle, far, own_kv, other_kv, queries, *refs):
    atts, before, wos, outs, (got, held, loaded, sems) = refs[0], refs[1], refs[2:4], refs[4:8], refs[8:]
    loads = loads_of(wos, loaded, sems)
    for load in sum(loads, []):
        load.start()
    z, core = pos[0], pos[1]
    x = jnp.where((z == 1) | (z == 2), middle[...], far[...])
    attention(z ^ 3, core, counts, x, (own_kv, other_kv), queries, got)
    held[0] = before[...]
    for flip in range(4):
        held[(z ^ flip) + 1] = got[...] if flip == 3 else atts[flip]
    first = lax.broadcasted_iota(jnp.int32, got.shape, 0) == 0
    rows = []
    for flip in range(4):
        i = (z ^ flip) + 1
        rows.append(jnp.where(first, held[i], held[i - core]))
    rows = jnp.concatenate(rows, axis=0)
    piece = loaded.shape[2]
    for p, pair in enumerate(loads):
        for load in pair:
            load.wait()
        result = dot(rows, loaded[p]).astype(BF16)
        for flip in range(4):
            outs[flip][:, pl.ds(p * piece, piece)] = result[flip * GROUP : (flip + 1) * GROUP]


def last_attend(pos, counts, middle, far, wkvs, queries, atts, before, wos):
    keys, width = middle.shape
    heads, model = wos[0].shape
    pieces = 4
    return pl.pallas_call(
        last_kernel,
        in_specs=[SMEM, SMEM] + [VMEM] * 7 + [HBM, ANY],
        out_specs=[VMEM] * 5,
        out_shape=[jax.ShapeDtypeStruct((GROUP, model), BF16)] * 4 + [jax.ShapeDtypeStruct(before.shape, BF16)],
        scratch_shapes=[
            pltpu.VMEM((5,) + before.shape, BF16),
            pltpu.VMEM((pieces, 2 * heads, model // pieces), BF16),
            pltpu.SemaphoreType.DMA((2, pieces)),
        ],
        compiler_params=params(),
        cost_estimate=pl.CostEstimate(
            flops=16 * GROUP * heads * model + 8 * keys * heads * (width + GROUP),
            bytes_accessed=4 * heads * model + 8 * GROUP * model,
            transcendentals=2 * GROUP * keys * heads // HEAD_DIM,
        ),
        name="last_attend",
    )(pos, counts, middle, far, *wkvs, queries, atts, before, *wos)


def late_kernel(before, own_w, other_w, out, loaded, sems):
    loads = loads_of((own_w, other_w), loaded, sems)
    for load in sum(loads, []):
        load.start()
    first = lax.broadcasted_iota(jnp.int32, before.shape, 0) == 0
    rows = jnp.where(first, 0.0, before[...].astype(F32)).astype(BF16)
    piece = loaded.shape[2]
    for p, pair in enumerate(loads):
        for load in pair:
            load.wait()
        out[:, pl.ds(p * piece, piece)] = dot(rows, loaded[p]).astype(BF16)


def late_out(before, wos):
    heads, model = wos[0].shape
    pieces = 4
    return pl.pallas_call(
        late_kernel,
        in_specs=[VMEM, HBM, ANY],
        out_specs=VMEM,
        out_shape=jax.ShapeDtypeStruct((GROUP, model), BF16),
        scratch_shapes=[
            pltpu.VMEM((pieces, 2 * heads, model // pieces), BF16),
            pltpu.SemaphoreType.DMA((2, pieces)),
        ],
        compiler_params=params(),
        cost_estimate=pl.CostEstimate(
            flops=4 * GROUP * heads * model, bytes_accessed=4 * heads * model, transcendentals=0
        ),
        name="late_out",
    )(before, *wos)


def by_groups(
    tokens,
    nbr_embed,
    neighbour_table,
    valid_counts,
    dec_proj,
    enc_query,
    enc_out,
    enc_gain,
    nbr_proj,
    out_proj,
):
    nz = lax.axis_size("nbr") // 2
    n_seq = lax.axis_size("seq")
    seq_index = lax.axis_index("seq")
    member = lax.axis_index("nbr")
    z, core = member // 2, member % 2
    pos = jnp.stack([z, core]).astype(jnp.int32)
    width = dec_proj.shape[2]
    ch_grp, slots = neighbour_table.shape
    nb_grp, share, enc_width = nbr_embed.shape

    ids = neighbour_table.reshape(nz, 2, slots) - seq_index * nb_grp

    def picked(c):
        mine = lax.dynamic_index_in_dim(ids, c, 1, False).reshape(-1)
        return jnp.take(nbr_embed, mine, axis=0, mode="clip").reshape(nz, slots * share, enc_width)

    held = lax.optimization_barrier

    two, one = hop(tokens, 2), hop(tokens, 1)
    nbr_own = jnp.stack([picked(core), swapped(picked(1 - core), nz)])
    two, one, own, nbr_own, enc_query, enc_out, nbr_proj, out_proj = held(
        (two, one, tokens, nbr_own, enc_query, enc_out, nbr_proj, out_proj)
    )
    far, middle = hop(two, 1, MIDDLE), hop(own, 3, MIDDLE)
    wkv = nbr_proj.reshape(enc_width, 2 * width)
    encos, wkvs, outps = [(w, swapped(w, nz)) for w in (enc_out, wkv, out_proj)]
    column = jnp.stack([own, one, two, jnp.where((z == 1) | (z == 2), middle, far)])
    column, encos, wkvs, outps = held((column, encos, wkvs, outps))
    other = swapped(column, nz)
    encqs = (enc_query, swapped(enc_query, nz))
    nbr_two, nbr_one = hop(nbr_own, 2), hop(nbr_own, 1)
    mine, theirs = project(pos, column, other, dec_proj.transpose(1, 0, 2))
    mine, theirs, nbr_two, nbr_one, nbr_own, encqs = held((mine, theirs, nbr_two, nbr_one, nbr_own, encqs))
    nbrs = (nbr_own, nbr_one, nbr_two, hop(nbr_own, 3, MIDDLE), hop(nbr_two, 1, MIDDLE))
    projected = [p.reshape(nz * GROUP, 3 * width) for p in (mine, swapped(theirs, nz))]

    last = jnp.concatenate([p[:, :width].reshape(nz, GROUP, width)[:, GROUP - 1 :] for p in projected], axis=2)
    others = jnp.concatenate([theirs[:, :, :width], swapped(mine[:, :, :width], nz)], axis=2)
    queries = jnp.concatenate([last, others[:, : GROUP - 1]], axis=1)
    odd = range(1, 2 * nz, 2)
    back = [((q + 1) * 2 * nz + n, q * 2 * nz + n) for q in range(n_seq - 1) for n in odd]
    queries = jnp.concatenate([queries, lax.ppermute(queries[:1], ("seq", "nbr"), back)])
    counts = lax.dynamic_index_in_dim(
        lax.dynamic_slice_in_dim(valid_counts, seq_index * ch_grp, ch_grp, 0).reshape(nz, 2), core, 1, False
    )

    nbrs, queries = held((nbrs, queries))
    raws = []

    def part(flips):
        got = encode(pos, nbrs, flips, encqs, projected, encos)
        raws.extend(got[len(flips) :])
        return got[: len(flips)]

    arrived = scattered(part)
    enc_own = normed(arrived, raws[0], enc_gain.reshape(1, -1))
    enc_two, enc_one = hop(enc_own, 2), hop(enc_own, 1)
    first = attend(pos, counts, (enc_own,), wkvs, queries)
    enc_two, enc_mine, first = held((enc_two, enc_own, first))
    enc_middle, enc_far = hop(enc_mine, 3, MIDDLE), hop(enc_two, 1, MIDDLE)
    atts = attend(pos, counts, (enc_one, enc_two), wkvs, queries, first)

    def onward(x, chips):
        route = [(q * 2 * nz + 2 * i + 1, (q + 1) * 2 * nz + 2 * i + 1) for q in range(n_seq - 1) for i in chips]
        got = lax.ppermute(x, ("seq", "nbr"), route)
        return jnp.where((seq_index * ch_grp * GROUP) % SEQ_LEN == 0, 0, got).astype(BF16)

    before = onward(atts[3], (1, 2, 3))
    *outs, last = last_attend(pos, counts, enc_middle, enc_far, wkvs, queries, atts, before, outps)
    arrived = scattered(lambda flips: [outs[flip] for flip in flips])
    arrived.append(late_out(onward(last, (0,)), outps))
    mine = sum(part.astype(F32) for part in arrived).astype(BF16)
    theirs = swapped(mine, nz)
    cross_out = jnp.concatenate([theirs[1:], mine[:1]], axis=0)

    encoded = enc_own.reshape(nz, 2, slots, share, enc_width)
    encoded = jnp.where(core == 0, encoded, encoded[:, ::-1]).transpose(2, 0, 1, 3, 4).reshape(-1, enc_width)
    return (cross_out, encoded)


def local(*args):
    tokens, table = args[0], args[2]
    chips = lax.axis_size("nbr") // 2
    if chips == 4 and table.shape[0] == 8 and tokens.shape[0] == GROUP:
        return by_groups(*args)
    return by_heads(*args)


def solution(mesh):
    return jax.shard_map(
        local,
        mesh=mesh,
        in_specs=(
            P(("seq", "nbr"), None),
            P("seq", "nbr", None),
            P("seq", None),
            P(),
            P(None, None, "nbr"),
            P(None, "nbr"),
            P("nbr", None),
            P(),
            P(None, None, "nbr"),
            P("nbr", None),
        ),
        out_specs=(P(("seq", "nbr"), None), P(("seq", "nbr"), None)),
        check_vma=False,
    )
```

```python
import functools

import jax
import jax.numpy as jnp
from jax import lax
from jax.experimental import pallas as pl
from jax.experimental.pallas import tpu as pltpu
from jax.sharding import PartitionSpec as P

HEAD_DIM = 128
GROUP = 64
NLEN = 128
SEQ_LEN = 2048
SCALE = 1.0 / HEAD_DIM**0.5
F32 = jnp.float32
BF16 = jnp.bfloat16
HBM = pl.BlockSpec(memory_space=pltpu.HBM)
ANY = pl.BlockSpec(memory_space=pl.ANY)
SMEM = pl.BlockSpec(memory_space=pltpu.SMEM)
VMEM = pl.BlockSpec(memory_space=pltpu.VMEM)


def passed_along(block, axis, distance):
    devices = range(lax.axis_size(axis))
    route = [(i - distance, i) for i in devices if i - distance in devices]
    return lax.ppermute(block, axis, route)


def plain_softmax(scores):
    peak = jnp.max(scores, axis=-1, keepdims=True)
    raised = jnp.exp(scores - peak)
    return (raised / jnp.sum(raised, axis=-1, keepdims=True)).astype(jnp.bfloat16)


def masked_softmax(scores, allowed):
    live = jnp.any(allowed, axis=-1, keepdims=True)
    peak = jnp.max(jnp.where(allowed, scores, -1e30), axis=-1, keepdims=True)
    peak = jnp.where(live, peak, 0.0)
    raised = jnp.where(allowed, jnp.exp(scores - peak), 0.0)
    denominator = jnp.where(live, jnp.sum(raised, axis=-1, keepdims=True), 1.0)
    return (raised / denominator).astype(jnp.bfloat16)


def normed_rows(raw_rows, partial_sum, enc_gain):
    combined = raw_rows.astype(jnp.float32) + partial_sum
    factor = lax.rsqrt(jnp.mean(combined * combined, axis=-1, keepdims=True) + 1e-06)
    return (combined * factor * enc_gain).astype(jnp.bfloat16)


def by_heads(
    tokens,
    nbr_embed,
    neighbour_table,
    valid_counts,
    dec_proj,
    enc_query,
    enc_out,
    enc_gain,
    nbr_proj,
    out_proj,
):
    n_nbr = lax.axis_size("nbr")
    seq_index = lax.axis_index("seq")
    member = lax.axis_index("nbr")
    model_width = tokens.shape[1]
    local_width = dec_proj.shape[2]
    head_dev = local_width // HEAD_DIM
    scale = 1.0 / HEAD_DIM**0.5
    dec_flat = dec_proj.reshape(model_width, 3 * local_width)
    projected = jnp.dot(
        lax.all_gather(tokens, "nbr", axis=0, tiled=True),
        dec_flat,
        preferred_element_type=jnp.float32,
    ).astype(jnp.bfloat16)
    tok_grp = projected.shape[0]
    ch_grp = tok_grp // GROUP
    queries = projected[:, :local_width]
    cond_key = projected[:, local_width : 2 * local_width].reshape(
        ch_grp, GROUP, head_dev, HEAD_DIM
    )
    cond_value = projected[:, 2 * local_width :].reshape(ch_grp, GROUP, head_dev, HEAD_DIM)
    grp_embed = lax.all_gather(nbr_embed, "nbr", axis=1, tiled=True)
    nb_grp = grp_embed.shape[0]
    enc_width = grp_embed.shape[2]
    row_ids = neighbour_table.reshape(-1) - seq_index * nb_grp
    ordered = jnp.take(grp_embed, row_ids, axis=0).reshape(-1, enc_width)
    enc_queries = jnp.dot(ordered, enc_query, preferred_element_type=jnp.float32).astype(
        jnp.bfloat16
    )
    enc_queries = enc_queries.reshape(ch_grp, -1, head_dev, HEAD_DIM)
    enc_scores = (
        jnp.einsum("cqhd,ckhd->chqk", enc_queries, cond_key, preferred_element_type=jnp.float32)
        * scale
    )
    enc_weights = plain_softmax(enc_scores)
    enc_att = jnp.einsum(
        "chqk,ckhd->cqhd", enc_weights, cond_value, preferred_element_type=jnp.float32
    ).astype(jnp.bfloat16)
    enc_att = enc_att.reshape(-1, local_width)
    share_rows = enc_att.shape[0] // n_nbr
    summed = lax.psum(jnp.dot(enc_att, enc_out, preferred_element_type=jnp.float32), "nbr")
    encoded_all = normed_rows(ordered, summed, enc_gain)
    encoded_mine = lax.dynamic_slice_in_dim(encoded_all, member * share_rows, share_rows, 0)
    nbr_kv = jnp.dot(
        encoded_all,
        nbr_proj.reshape(enc_width, 2 * local_width),
        preferred_element_type=jnp.float32,
    ).astype(jnp.bfloat16)
    nbr_kv = nbr_kv.reshape(ch_grp, -1, 2 * local_width)
    previous = passed_along(nbr_kv[-1], "seq", 1)
    kv_ext = jnp.concatenate([previous[None], nbr_kv], axis=0)
    key_rows = kv_ext.shape[1]
    kv_ext = kv_ext.reshape(ch_grp + 1, key_rows, 2, head_dev, HEAD_DIM)
    counts_pad = jnp.concatenate([jnp.zeros((1,), jnp.int32), valid_counts], axis=0)
    counts_ext = lax.dynamic_slice_in_dim(counts_pad, seq_index * ch_grp, ch_grp + 1, 0)
    query_pad = jnp.concatenate(
        [
            jnp.zeros((1, local_width), jnp.bfloat16),
            queries,
            jnp.zeros((GROUP - 1, local_width), jnp.bfloat16),
        ],
        axis=0,
    )
    query_pad = query_pad.reshape(ch_grp + 1, GROUP, head_dev, HEAD_DIM)
    local_ids = jnp.arange((ch_grp + 1) * GROUP, dtype=jnp.int32) - 1
    global_ids = seq_index * tok_grp + local_ids
    active = (local_ids >= 0) & (local_ids < tok_grp) & (global_ids % SEQ_LEN >= GROUP - 1)
    active = active.reshape(ch_grp + 1, GROUP)
    key_slot = jnp.arange(key_rows, dtype=jnp.int32) // NLEN
    slot_live = key_slot[None, :] < counts_ext[:, None]
    allowed = active[:, None, :, None] & slot_live[:, None, None, :]
    cca_scores = (
        jnp.einsum(
            "bqhd,bkhd->bhqk", query_pad, kv_ext[:, :, 0], preferred_element_type=jnp.float32
        )
        * scale
    )
    cca_weights = masked_softmax(cca_scores, allowed)
    cca_att = jnp.einsum(
        "bhqk,bkhd->bqhd", cca_weights, kv_ext[:, :, 1], preferred_element_type=jnp.float32
    ).astype(jnp.bfloat16)
    cca_att = cca_att.reshape(-1, local_width)[1 : tok_grp + 1]
    cross_out = lax.psum_scatter(
        jnp.dot(cca_att, out_proj, preferred_element_type=jnp.float32).astype(jnp.bfloat16),
        "nbr",
        scatter_dimension=0,
        tiled=True,
    )
    return (cross_out, encoded_mine)


def params():
    return pltpu.CompilerParams(vmem_limit_bytes=44 * 1024 * 1024)


def dot(a, b):
    return jnp.dot(a, b, preferred_element_type=F32)


def dot_t(a, b):
    return lax.dot_general(a, b, (((1,), (1,)), ((), ())), preferred_element_type=F32)


def swapped(x, nz):
    return lax.ppermute(x, "nbr", [(n, n ^ 1) for n in range(2 * nz)])


ENDS, MIDDLE = (0, 3), (1, 2)


def hop(x, flip, chips=(0, 1, 2, 3)):
    return lax.ppermute(x, "nbr", [(2 * z + c, 2 * (z ^ flip) + c) for z in chips for c in range(2)])


def scattered(part):
    two, three = part((2, 3))
    outer = hop(two, 2, ENDS)
    passed, middle = hop(three, 1, ENDS), hop(three, 3, MIDDLE)
    one, own = part((1, 0))
    one = hop(one, 1)
    inner = hop((two.astype(F32) + passed.astype(F32)).astype(BF16), 2, MIDDLE)
    return [own, one, outer, inner, middle]


def fetches(pos, parts, place, sems):
    inside = (pos[0] == 1) | (pos[0] == 2)
    when = [None, None, None, inside, jnp.logical_not(inside)]
    k = 0
    jobs = []
    for ref, ok, flip in zip(parts, when, (0, 1, 2, 3, 3)):
        for src, dst in place(ref, pos[0] ^ flip):
            jobs.append((ok, pltpu.make_async_copy(src, dst, sems.at[k])))
            k += 1
    return jobs


def each(jobs, act):
    for ok, job in jobs:
        if ok is None:
            act(job)
        else:
            pl.when(ok)(functools.partial(act, job))


def begin(jobs):
    each(jobs, lambda job: job.start())


def finish(jobs):
    each(jobs, lambda job: job.wait())


def proj_kernel(pos, own, other, w, mine, theirs, held, sems):
    pieces, depth, width = held.shape
    loads = [pltpu.make_async_copy(w.at[p], held.at[p], sems.at[p]) for p in range(pieces)]
    for load in loads:
        load.start()
    rows = jnp.concatenate([own[...].reshape(-1, depth), other[...].reshape(-1, depth)], axis=0)
    for p in range(pieces):
        loads[p].wait()
        got = dot(rows, held[p]).astype(BF16).reshape(2, 4, GROUP, width)
        for c, out in enumerate((mine, theirs)):
            for flip in range(4):
                out[pos[0] ^ flip, :, pl.ds(p * width, width)] = got[c, flip]


def project(pos, own, other, w):
    _, rows, depth = own.shape
    pieces, _, width = w.shape
    shape = jax.ShapeDtypeStruct((4, rows, pieces * width), BF16)
    return pl.pallas_call(
        proj_kernel,
        in_specs=[SMEM, VMEM, VMEM, HBM],
        out_specs=[VMEM, VMEM],
        out_shape=[shape, shape],
        scratch_shapes=[pltpu.VMEM(w.shape, BF16), pltpu.SemaphoreType.DMA((pieces,))],
        compiler_params=params(),
        cost_estimate=pl.CostEstimate(
            flops=16 * rows * depth * width * pieces,
            bytes_accessed=2 * depth * (width * pieces + 8 * rows),
            transcendentals=0,
        ),
        name="project",
    )(pos, own, other, w)


def enc_kernel(ahead, pos, *refs):
    parts, weights, refs = refs[:5], (refs[5:9], refs[9:13]), refs[13:]
    if ahead:
        (two, three, one, own, raw), refs = refs[:5], refs[5:]
    else:
        (one, own, raw), refs = refs[3:6], refs[6:]
    rows, att, sems = refs
    shape = own.shape

    def work(flips, outs):
        n = len(flips)
        for act in begin, finish:
            for k, flip in enumerate(flips):
                i = pos[0] ^ flip
                place = lambda ref, j: [(ref.at[c, i], rows.at[k, j, c]) for c in range(2)]
                act(fetches(pos, parts, place, sems.at[k]))
        x = rows[...].reshape(n * shape[0], shape[1])
        if flips[-1] == 0:
            raw[...] = x[(n - 1) * shape[0] :]
        heads = weights[0][0].shape[1]
        qs = [dot(x, wq[...]).astype(BF16) for wq, *_ in weights]
        chains = [(w, c, h) for w in range(2) for c in range(n) for h in range(0, heads, HEAD_DIM)]
        here = [pl.ds(pl.multiple_of((pos[0] ^ flip) * GROUP, GROUP), GROUP) for flip in flips]
        scores = []
        for w, c, h in chains:
            ask = qs[w][c * shape[0] : (c + 1) * shape[0], h : h + HEAD_DIM]
            scores.append(dot_t(weights[w][1][here[c], pl.ds(h, HEAD_DIM)], ask)[None])
        scores = jnp.concatenate(scores, axis=0) * SCALE
        raised = jnp.exp(scores - jnp.max(scores, axis=1, keepdims=True))
        share = (raised / jnp.sum(raised, axis=1, keepdims=True)).astype(BF16)
        for m, (w, c, h) in enumerate(chains):
            att[pl.ds(c * shape[0], shape[0]), pl.ds(w * heads + h, HEAD_DIM)] = lax.dot_general(
                share[m],
                weights[w][2][here[c], pl.ds(h, HEAD_DIM)],
                (((0,), (0,)), ((), ())),
                preferred_element_type=F32,
            ).astype(BF16)
        total = dot(att[:, pl.ds(0, heads)], weights[0][3][...]) + dot(att[:, pl.ds(heads, heads)], weights[1][3][...])
        for k, out in enumerate(outs):
            out[...] = total[k * shape[0] : (k + 1) * shape[0]].astype(BF16)

    if ahead:
        work((2, 3), (two, three))
    pl.when(pos[1] == (0 if ahead else 1))(lambda: work((1, 0), (one, own)))


def encode(pos, parts, queries, projected, outs, *results):
    _, _, part, width = parts[0].shape
    tokens = projected[0].shape[0]
    heads = queries[0].shape[1]
    rows = 8 * part
    kv = [pl.BlockSpec((tokens, heads), lambda i: (0, 1)), pl.BlockSpec((tokens, heads), lambda i: (0, 2))]
    args = []
    for wq, proj, wo in zip(queries, projected, outs):
        args += [wq, proj, proj, wo]
    ahead = not results
    n = 5 if ahead else 3
    return pl.pallas_call(
        functools.partial(enc_kernel, ahead),
        grid=(1,),
        in_specs=[SMEM] + [ANY] * 5 + ([VMEM] + kv + [VMEM]) * 2 + [VMEM] * len(results),
        out_specs=[VMEM] * n,
        out_shape=[jax.ShapeDtypeStruct((rows, width), BF16)] * n,
        input_output_aliases={14 + i: i for i in range(len(results))},
        scratch_shapes=[
            pltpu.VMEM((2, 4, 2, part, width), BF16),
            pltpu.VMEM((2 * rows, 2 * heads), BF16),
            pltpu.SemaphoreType.DMA((2, 10)),
        ],
        compiler_params=params(),
        cost_estimate=pl.CostEstimate(
            flops=4 * rows * heads * (4 * width + 4 * GROUP),
            bytes_accessed=8 * rows * width + 8 * heads * width,
            transcendentals=2 * rows * heads,
        ),
        name="encode",
    )(pos, *parts, *args, *results)


def norm_kernel(nz, *refs):
    raw, gain, out = refs[nz:]
    combined = raw[...].astype(F32) + sum(r[...].astype(F32) for r in refs[:nz])
    factor = lax.rsqrt(jnp.mean(combined * combined, axis=-1, keepdims=True) + 1e-06)
    out[...] = (combined * factor * gain[...]).astype(BF16)


def normed(parts, raw, gain):
    return pl.pallas_call(
        functools.partial(norm_kernel, len(parts)),
        in_specs=[VMEM] * (len(parts) + 2),
        out_specs=VMEM,
        out_shape=jax.ShapeDtypeStruct(raw.shape, BF16),
        compiler_params=params(),
        name="normed",
    )(*parts, raw, gain)


def attention(i, core, counts, x, wkvs, queries, out):
    keys, heads = x.shape[0], wkvs[0].shape[1] // 2
    slot = lax.broadcasted_iota(jnp.int32, (GROUP, keys), 1) // (keys // 16) % 2
    first = lax.broadcasted_iota(jnp.int32, (GROUP, 2 * heads), 0) == 0
    allowed = slot < counts[i]
    q = jnp.where(first, queries[i], queries[i + core])
    kvs = [dot(x, wkv[...]).astype(BF16) for wkv in wkvs]
    each_head = [(w, h) for w in range(2) for h in range(0, heads, HEAD_DIM)]
    scores = [
        dot_t(q[:, heads * w + h : heads * w + h + HEAD_DIM], kvs[w][:, h : h + HEAD_DIM]) for w, h in each_head
    ]
    scores = jnp.concatenate(scores, axis=0) * SCALE
    allowed = jnp.concatenate([allowed] * len(each_head), axis=0)
    scores = jnp.where(allowed, scores, -1e30)
    raised = jnp.where(allowed, jnp.exp(scores - jnp.max(scores, axis=-1, keepdims=True)), 0.0)
    share = (raised / jnp.sum(raised, axis=-1, keepdims=True)).astype(BF16)
    for k, (w, h) in enumerate(each_head):
        value = kvs[w][:, heads + h : heads + h + HEAD_DIM]
        out[:, pl.ds(heads * w + h, HEAD_DIM)] = dot(share[k * GROUP : (k + 1) * GROUP], value).astype(BF16)


def attend_kernel(pos, counts, rows, own_kv, other_kv, queries, out):
    attention(pos[0], pos[1], counts, rows[...], (own_kv, other_kv), queries, out)


def attend_more_kernel(pos, counts, one, two, own_kv, other_kv, queries, first, out, pick):
    out[0] = first[...]
    for flip, x in (1, one), (2, two):
        attention(pos[0] ^ flip, pos[1], counts, x[...], (own_kv, other_kv), queries, out.at[flip])
    z = pos[0]
    pick[...] = jnp.where(z == 3, out[0], jnp.where(z == 2, out[1], out[2]))


def attend(pos, counts, rows, wkvs, queries, *earlier):
    keys, width = rows[0].shape
    both = wkvs[0].shape[1]
    n = len(rows)
    single = jax.ShapeDtypeStruct((GROUP, both), BF16)
    return pl.pallas_call(
        attend_more_kernel if earlier else attend_kernel,
        in_specs=[SMEM, SMEM] + [VMEM] * (n + 3 + len(earlier)),
        out_specs=[VMEM, VMEM] if earlier else VMEM,
        out_shape=[jax.ShapeDtypeStruct((3, GROUP, both), BF16), single] if earlier else single,
        compiler_params=params(),
        cost_estimate=pl.CostEstimate(
            flops=4 * n * keys * both * (width + GROUP),
            bytes_accessed=2 * (2 * width * both + n * keys * width),
            transcendentals=n * GROUP * keys * both // HEAD_DIM,
        ),
        name="attend",
    )(pos, counts, *rows, *wkvs, queries, *earlier)


def loads_of(wos, loaded, sems):
    heads, model = wos[0].shape
    pieces = sems.shape[1]
    piece = model // pieces
    return [
        [
            pltpu.make_async_copy(
                wos[w].at[:, pl.ds(p * piece, piece)], loaded.at[p, pl.ds(w * heads, heads)], sems.at[w, p]
            )
            for w in range(2)
        ]
        for p in range(pieces)
    ]


def last_kernel(pos, counts, middle, far, own_kv, other_kv, queries, *refs):
    atts, before, wos, outs, (got, held, loaded, sems) = refs[0], refs[1], refs[2:4], refs[4:8], refs[8:]
    loads = loads_of(wos, loaded, sems)
    for load in sum(loads, []):
        load.start()
    z, core = pos[0], pos[1]
    x = jnp.where((z == 1) | (z == 2), middle[...], far[...])
    attention(z ^ 3, core, counts, x, (own_kv, other_kv), queries, got)
    held[0] = before[...]
    for flip in range(4):
        held[(z ^ flip) + 1] = got[...] if flip == 3 else atts[flip]
    first = lax.broadcasted_iota(jnp.int32, got.shape, 0) == 0
    rows = []
    for flip in range(4):
        i = (z ^ flip) + 1
        rows.append(jnp.where(first, held[i], held[i - core]))
    rows = jnp.concatenate(rows, axis=0)
    piece = loaded.shape[2]
    for p, pair in enumerate(loads):
        for load in pair:
            load.wait()
        result = dot(rows, loaded[p]).astype(BF16)
        for flip in range(4):
            outs[flip][:, pl.ds(p * piece, piece)] = result[flip * GROUP : (flip + 1) * GROUP]


def last_attend(pos, counts, middle, far, wkvs, queries, atts, before, wos):
    keys, width = middle.shape
    heads, model = wos[0].shape
    pieces = 4
    return pl.pallas_call(
        last_kernel,
        in_specs=[SMEM, SMEM] + [VMEM] * 7 + [HBM, ANY],
        out_specs=[VMEM] * 5,
        out_shape=[jax.ShapeDtypeStruct((GROUP, model), BF16)] * 4 + [jax.ShapeDtypeStruct(before.shape, BF16)],
        scratch_shapes=[
            pltpu.VMEM((5,) + before.shape, BF16),
            pltpu.VMEM((pieces, 2 * heads, model // pieces), BF16),
            pltpu.SemaphoreType.DMA((2, pieces)),
        ],
        compiler_params=params(),
        cost_estimate=pl.CostEstimate(
            flops=16 * GROUP * heads * model + 8 * keys * heads * (width + GROUP),
            bytes_accessed=4 * heads * model + 8 * GROUP * model,
            transcendentals=2 * GROUP * keys * heads // HEAD_DIM,
        ),
        name="last_attend",
    )(pos, counts, middle, far, *wkvs, queries, atts, before, *wos)


def late_kernel(before, own_w, other_w, out, loaded, sems):
    loads = loads_of((own_w, other_w), loaded, sems)
    for load in sum(loads, []):
        load.start()
    first = lax.broadcasted_iota(jnp.int32, before.shape, 0) == 0
    rows = jnp.where(first, 0.0, before[...].astype(F32)).astype(BF16)
    piece = loaded.shape[2]
    for p, pair in enumerate(loads):
        for load in pair:
            load.wait()
        out[:, pl.ds(p * piece, piece)] = dot(rows, loaded[p]).astype(BF16)


def late_out(before, wos):
    heads, model = wos[0].shape
    pieces = 4
    return pl.pallas_call(
        late_kernel,
        in_specs=[VMEM, HBM, ANY],
        out_specs=VMEM,
        out_shape=jax.ShapeDtypeStruct((GROUP, model), BF16),
        scratch_shapes=[
            pltpu.VMEM((pieces, 2 * heads, model // pieces), BF16),
            pltpu.SemaphoreType.DMA((2, pieces)),
        ],
        compiler_params=params(),
        cost_estimate=pl.CostEstimate(
            flops=4 * GROUP * heads * model, bytes_accessed=4 * heads * model, transcendentals=0
        ),
        name="late_out",
    )(before, *wos)


def by_groups(
    tokens,
    nbr_embed,
    neighbour_table,
    valid_counts,
    dec_proj,
    enc_query,
    enc_out,
    enc_gain,
    nbr_proj,
    out_proj,
):
    nz = lax.axis_size("nbr") // 2
    n_seq = lax.axis_size("seq")
    seq_index = lax.axis_index("seq")
    member = lax.axis_index("nbr")
    z, core = member // 2, member % 2
    pos = jnp.stack([z, core]).astype(jnp.int32)
    width = dec_proj.shape[2]
    ch_grp, slots = neighbour_table.shape
    nb_grp, share, enc_width = nbr_embed.shape

    ids = neighbour_table.reshape(nz, 2, slots) - seq_index * nb_grp

    def picked(c):
        mine = lax.dynamic_index_in_dim(ids, c, 1, False).reshape(-1)
        return jnp.take(nbr_embed, mine, axis=0, mode="clip").reshape(nz, slots * share, enc_width)

    held = lax.optimization_barrier

    two, one = hop(tokens, 2), hop(tokens, 1)
    nbr_own = jnp.stack([picked(core), swapped(picked(1 - core), nz)])
    two, one, own, nbr_own, enc_query, enc_out, nbr_proj, out_proj = held(
        (two, one, tokens, nbr_own, enc_query, enc_out, nbr_proj, out_proj)
    )
    far, middle = hop(two, 1, MIDDLE), hop(own, 3, MIDDLE)
    wkv = nbr_proj.reshape(enc_width, 2 * width)
    encos, wkvs, outps = [(w, swapped(w, nz)) for w in (enc_out, wkv, out_proj)]
    column = jnp.stack([own, one, two, jnp.where((z == 1) | (z == 2), middle, far)])
    column, encos, wkvs, outps = held((column, encos, wkvs, outps))
    other = swapped(column, nz)
    encqs = (enc_query, swapped(enc_query, nz))
    nbr_two, nbr_one = hop(nbr_own, 2), hop(nbr_own, 1)
    mine, theirs = project(pos, column, other, dec_proj.transpose(1, 0, 2))
    mine, theirs, nbr_two, nbr_one, nbr_own, encqs = held((mine, theirs, nbr_two, nbr_one, nbr_own, encqs))
    nbrs = (nbr_own, nbr_one, nbr_two, hop(nbr_own, 3, MIDDLE), hop(nbr_two, 1, MIDDLE))
    projected = [p.reshape(nz * GROUP, 3 * width) for p in (mine, swapped(theirs, nz))]

    last = jnp.concatenate([p[:, :width].reshape(nz, GROUP, width)[:, GROUP - 1 :] for p in projected], axis=2)
    others = jnp.concatenate([theirs[:, :, :width], swapped(mine[:, :, :width], nz)], axis=2)
    counts = lax.dynamic_index_in_dim(
        lax.dynamic_slice_in_dim(valid_counts, seq_index * ch_grp, ch_grp, 0).reshape(nz, 2), core, 1, False
    )

    nbrs, others, last = held((nbrs, others, last))
    queries = jnp.concatenate([last, others[:, : GROUP - 1]], axis=1)
    odd = range(1, 2 * nz, 2)
    back = [((q + 1) * 2 * nz + n, q * 2 * nz + n) for q in range(n_seq - 1) for n in odd]
    queries = jnp.concatenate([queries, lax.ppermute(queries[:1], ("seq", "nbr"), back)])
    two, three, *rest = encode(pos, nbrs, encqs, projected, encos)
    raws = []

    def part(flips):
        if flips == (2, 3):
            return two, three
        one, own, raw = encode(pos, nbrs, encqs, projected, encos, *rest)
        raws.append(raw)
        return one, own

    arrived = scattered(part)
    enc_own = normed(arrived, raws[0], enc_gain.reshape(1, -1))
    enc_two, enc_one = hop(enc_own, 2), hop(enc_own, 1)
    first = attend(pos, counts, (enc_own,), wkvs, queries)
    enc_two, enc_mine, first = held((enc_two, enc_own, first))
    enc_middle, enc_far = hop(enc_mine, 3, MIDDLE), hop(enc_two, 1, MIDDLE)
    atts, pick = attend(pos, counts, (enc_one, enc_two), wkvs, queries, first)

    def onward(x, chips):
        route = [(q * 2 * nz + 2 * i + 1, (q + 1) * 2 * nz + 2 * i + 1) for q in range(n_seq - 1) for i in chips]
        got = lax.ppermute(x, ("seq", "nbr"), route)
        return jnp.where((seq_index * ch_grp * GROUP) % SEQ_LEN == 0, 0, got).astype(BF16)

    before = onward(pick, (1, 2, 3))
    *outs, last = last_attend(pos, counts, enc_middle, enc_far, wkvs, queries, atts, before, outps)
    arrived = scattered(lambda flips: [outs[flip] for flip in flips])
    arrived.append(late_out(onward(last, (0,)), outps))
    mine = sum(part.astype(F32) for part in arrived).astype(BF16)
    theirs = swapped(mine, nz)
    cross_out = jnp.concatenate([theirs[1:], mine[:1]], axis=0)

    encoded = enc_own.reshape(nz, 2, slots, share, enc_width)
    encoded = jnp.where(core == 0, encoded, encoded[:, ::-1]).transpose(2, 0, 1, 3, 4).reshape(-1, enc_width)
    return (cross_out, encoded)


def local(*args):
    tokens, table = args[0], args[2]
    chips = lax.axis_size("nbr") // 2
    if chips == 4 and table.shape[0] == 8 and tokens.shape[0] == GROUP:
        return by_groups(*args)
    return by_heads(*args)


def solution(mesh):
    return jax.shard_map(
        local,
        mesh=mesh,
        in_specs=(
            P(("seq", "nbr"), None),
            P("seq", "nbr", None),
            P("seq", None),
            P(),
            P(None, None, "nbr"),
            P(None, "nbr"),
            P("nbr", None),
            P(),
            P(None, None, "nbr"),
            P("nbr", None),
        ),
        out_specs=(P(("seq", "nbr"), None), P(("seq", "nbr"), None)),
        check_vma=False,
    )
```

```python
import functools

import jax
import jax.numpy as jnp
from jax import lax
from jax.experimental import pallas as pl
from jax.experimental.pallas import tpu as pltpu
from jax.sharding import PartitionSpec as P

HEAD_DIM = 128
GROUP = 64
NLEN = 128
SEQ_LEN = 2048
SCALE = 1.0 / HEAD_DIM**0.5
F32 = jnp.float32
BF16 = jnp.bfloat16
HBM = pl.BlockSpec(memory_space=pltpu.HBM)
ANY = pl.BlockSpec(memory_space=pl.ANY)
SMEM = pl.BlockSpec(memory_space=pltpu.SMEM)
VMEM = pl.BlockSpec(memory_space=pltpu.VMEM)


def passed_along(block, axis, distance):
    devices = range(lax.axis_size(axis))
    route = [(i - distance, i) for i in devices if i - distance in devices]
    return lax.ppermute(block, axis, route)


def plain_softmax(scores):
    peak = jnp.max(scores, axis=-1, keepdims=True)
    raised = jnp.exp(scores - peak)
    return (raised / jnp.sum(raised, axis=-1, keepdims=True)).astype(jnp.bfloat16)


def masked_softmax(scores, allowed):
    live = jnp.any(allowed, axis=-1, keepdims=True)
    peak = jnp.max(jnp.where(allowed, scores, -1e30), axis=-1, keepdims=True)
    peak = jnp.where(live, peak, 0.0)
    raised = jnp.where(allowed, jnp.exp(scores - peak), 0.0)
    denominator = jnp.where(live, jnp.sum(raised, axis=-1, keepdims=True), 1.0)
    return (raised / denominator).astype(jnp.bfloat16)


def normed_rows(raw_rows, partial_sum, enc_gain):
    combined = raw_rows.astype(jnp.float32) + partial_sum
    factor = lax.rsqrt(jnp.mean(combined * combined, axis=-1, keepdims=True) + 1e-06)
    return (combined * factor * enc_gain).astype(jnp.bfloat16)


def by_heads(
    tokens,
    nbr_embed,
    neighbour_table,
    valid_counts,
    dec_proj,
    enc_query,
    enc_out,
    enc_gain,
    nbr_proj,
    out_proj,
):
    n_nbr = lax.axis_size("nbr")
    seq_index = lax.axis_index("seq")
    member = lax.axis_index("nbr")
    model_width = tokens.shape[1]
    local_width = dec_proj.shape[2]
    head_dev = local_width // HEAD_DIM
    scale = 1.0 / HEAD_DIM**0.5
    dec_flat = dec_proj.reshape(model_width, 3 * local_width)
    projected = jnp.dot(
        lax.all_gather(tokens, "nbr", axis=0, tiled=True),
        dec_flat,
        preferred_element_type=jnp.float32,
    ).astype(jnp.bfloat16)
    tok_grp = projected.shape[0]
    ch_grp = tok_grp // GROUP
    queries = projected[:, :local_width]
    cond_key = projected[:, local_width : 2 * local_width].reshape(
        ch_grp, GROUP, head_dev, HEAD_DIM
    )
    cond_value = projected[:, 2 * local_width :].reshape(ch_grp, GROUP, head_dev, HEAD_DIM)
    grp_embed = lax.all_gather(nbr_embed, "nbr", axis=1, tiled=True)
    nb_grp = grp_embed.shape[0]
    enc_width = grp_embed.shape[2]
    row_ids = neighbour_table.reshape(-1) - seq_index * nb_grp
    ordered = jnp.take(grp_embed, row_ids, axis=0).reshape(-1, enc_width)
    enc_queries = jnp.dot(ordered, enc_query, preferred_element_type=jnp.float32).astype(
        jnp.bfloat16
    )
    enc_queries = enc_queries.reshape(ch_grp, -1, head_dev, HEAD_DIM)
    enc_scores = (
        jnp.einsum("cqhd,ckhd->chqk", enc_queries, cond_key, preferred_element_type=jnp.float32)
        * scale
    )
    enc_weights = plain_softmax(enc_scores)
    enc_att = jnp.einsum(
        "chqk,ckhd->cqhd", enc_weights, cond_value, preferred_element_type=jnp.float32
    ).astype(jnp.bfloat16)
    enc_att = enc_att.reshape(-1, local_width)
    share_rows = enc_att.shape[0] // n_nbr
    summed = lax.psum(jnp.dot(enc_att, enc_out, preferred_element_type=jnp.float32), "nbr")
    encoded_all = normed_rows(ordered, summed, enc_gain)
    encoded_mine = lax.dynamic_slice_in_dim(encoded_all, member * share_rows, share_rows, 0)
    nbr_kv = jnp.dot(
        encoded_all,
        nbr_proj.reshape(enc_width, 2 * local_width),
        preferred_element_type=jnp.float32,
    ).astype(jnp.bfloat16)
    nbr_kv = nbr_kv.reshape(ch_grp, -1, 2 * local_width)
    previous = passed_along(nbr_kv[-1], "seq", 1)
    kv_ext = jnp.concatenate([previous[None], nbr_kv], axis=0)
    key_rows = kv_ext.shape[1]
    kv_ext = kv_ext.reshape(ch_grp + 1, key_rows, 2, head_dev, HEAD_DIM)
    counts_pad = jnp.concatenate([jnp.zeros((1,), jnp.int32), valid_counts], axis=0)
    counts_ext = lax.dynamic_slice_in_dim(counts_pad, seq_index * ch_grp, ch_grp + 1, 0)
    query_pad = jnp.concatenate(
        [
            jnp.zeros((1, local_width), jnp.bfloat16),
            queries,
            jnp.zeros((GROUP - 1, local_width), jnp.bfloat16),
        ],
        axis=0,
    )
    query_pad = query_pad.reshape(ch_grp + 1, GROUP, head_dev, HEAD_DIM)
    local_ids = jnp.arange((ch_grp + 1) * GROUP, dtype=jnp.int32) - 1
    global_ids = seq_index * tok_grp + local_ids
    active = (local_ids >= 0) & (local_ids < tok_grp) & (global_ids % SEQ_LEN >= GROUP - 1)
    active = active.reshape(ch_grp + 1, GROUP)
    key_slot = jnp.arange(key_rows, dtype=jnp.int32) // NLEN
    slot_live = key_slot[None, :] < counts_ext[:, None]
    allowed = active[:, None, :, None] & slot_live[:, None, None, :]
    cca_scores = (
        jnp.einsum(
            "bqhd,bkhd->bhqk", query_pad, kv_ext[:, :, 0], preferred_element_type=jnp.float32
        )
        * scale
    )
    cca_weights = masked_softmax(cca_scores, allowed)
    cca_att = jnp.einsum(
        "bhqk,bkhd->bqhd", cca_weights, kv_ext[:, :, 1], preferred_element_type=jnp.float32
    ).astype(jnp.bfloat16)
    cca_att = cca_att.reshape(-1, local_width)[1 : tok_grp + 1]
    cross_out = lax.psum_scatter(
        jnp.dot(cca_att, out_proj, preferred_element_type=jnp.float32).astype(jnp.bfloat16),
        "nbr",
        scatter_dimension=0,
        tiled=True,
    )
    return (cross_out, encoded_mine)


def params():
    return pltpu.CompilerParams(vmem_limit_bytes=44 * 1024 * 1024)


def dot(a, b):
    return jnp.dot(a, b, preferred_element_type=F32)


def dot_t(a, b):
    return lax.dot_general(a, b, (((1,), (1,)), ((), ())), preferred_element_type=F32)


def swapped(x, nz):
    return lax.ppermute(x, "nbr", [(n, n ^ 1) for n in range(2 * nz)])


ENDS, MIDDLE = (0, 3), (1, 2)


def hop(x, flip, chips=(0, 1, 2, 3)):
    return lax.ppermute(x, "nbr", [(2 * z + c, 2 * (z ^ flip) + c) for z in chips for c in range(2)])


def scattered(part):
    two, three = part((2, 3))
    outer = hop(two, 2, ENDS)
    passed, middle = hop(three, 1, ENDS), hop(three, 3, MIDDLE)
    one, own = part((1, 0))
    one = hop(one, 1)
    inner = hop((two.astype(F32) + passed.astype(F32)).astype(BF16), 2, MIDDLE)
    return [own, one, outer, inner, middle]


def fetches(pos, parts, place, sems):
    inside = (pos[0] == 1) | (pos[0] == 2)
    when = [None, None, None, inside, jnp.logical_not(inside)]
    k = 0
    jobs = []
    for ref, ok, flip in zip(parts, when, (0, 1, 2, 3, 3)):
        for src, dst in place(ref, pos[0] ^ flip):
            jobs.append((ok, pltpu.make_async_copy(src, dst, sems.at[k])))
            k += 1
    return jobs


def each(jobs, act):
    for ok, job in jobs:
        if ok is None:
            act(job)
        else:
            pl.when(ok)(functools.partial(act, job))


def begin(jobs):
    each(jobs, lambda job: job.start())


def finish(jobs):
    each(jobs, lambda job: job.wait())


def proj_kernel(pos, own, other, w, mine, theirs, held, sems):
    pieces, depth, width = held.shape
    loads = [pltpu.make_async_copy(w.at[p], held.at[p], sems.at[p]) for p in range(pieces)]
    for load in loads:
        load.start()
    rows = jnp.concatenate([own[...].reshape(-1, depth), other[...].reshape(-1, depth)], axis=0)
    for p in range(pieces):
        loads[p].wait()
        got = dot(rows, held[p]).astype(BF16).reshape(2, 4, GROUP, width)
        for c, out in enumerate((mine, theirs)):
            for flip in range(4):
                out[pos[0] ^ flip, :, pl.ds(p * width, width)] = got[c, flip]


def project(pos, own, other, w):
    _, rows, depth = own.shape
    pieces, _, width = w.shape
    shape = jax.ShapeDtypeStruct((4, rows, pieces * width), BF16)
    return pl.pallas_call(
        proj_kernel,
        in_specs=[SMEM, VMEM, VMEM, HBM],
        out_specs=[VMEM, VMEM],
        out_shape=[shape, shape],
        scratch_shapes=[pltpu.VMEM(w.shape, BF16), pltpu.SemaphoreType.DMA((pieces,))],
        compiler_params=params(),
        cost_estimate=pl.CostEstimate(
            flops=16 * rows * depth * width * pieces,
            bytes_accessed=2 * depth * (width * pieces + 8 * rows),
            transcendentals=0,
        ),
        name="project",
    )(pos, own, other, w)


def enc_kernel(ahead, pos, *refs):
    parts, weights, refs = refs[:5], (refs[5:9], refs[9:13]), refs[13:]
    if ahead:
        (two, three, one, own, raw), refs = refs[:5], refs[5:]
    else:
        (one, own, raw), refs = refs[3:6], refs[6:]
    rows, att, sems = refs
    shape = own.shape

    def work(flips, outs):
        n = len(flips)
        for act in begin, finish:
            for k, flip in enumerate(flips):
                i = pos[0] ^ flip
                place = lambda ref, j: [(ref.at[c, i], rows.at[k, j, c]) for c in range(2)]
                act(fetches(pos, parts, place, sems.at[k]))
        x = rows[...].reshape(n * shape[0], shape[1])
        if flips[-1] == 0:
            raw[...] = x[(n - 1) * shape[0] :]
        heads = weights[0][0].shape[1]
        qs = [dot(x, wq[...]).astype(BF16) for wq, *_ in weights]
        chains = [(w, c, h) for w in range(2) for c in range(n) for h in range(0, heads, HEAD_DIM)]
        here = [pl.ds(pl.multiple_of((pos[0] ^ flip) * GROUP, GROUP), GROUP) for flip in flips]
        scores = []
        for w, c, h in chains:
            ask = qs[w][c * shape[0] : (c + 1) * shape[0], h : h + HEAD_DIM]
            scores.append(dot_t(weights[w][1][here[c], pl.ds(h, HEAD_DIM)], ask)[None])
        scores = jnp.concatenate(scores, axis=0) * SCALE
        raised = jnp.exp(scores - jnp.max(scores, axis=1, keepdims=True))
        share = (raised / jnp.sum(raised, axis=1, keepdims=True)).astype(BF16)
        for m, (w, c, h) in enumerate(chains):
            att[pl.ds(c * shape[0], shape[0]), pl.ds(w * heads + h, HEAD_DIM)] = lax.dot_general(
                share[m],
                weights[w][2][here[c], pl.ds(h, HEAD_DIM)],
                (((0,), (0,)), ((), ())),
                preferred_element_type=F32,
            ).astype(BF16)
        total = dot(att[:, pl.ds(0, heads)], weights[0][3][...]) + dot(att[:, pl.ds(heads, heads)], weights[1][3][...])
        for k, out in enumerate(outs):
            out[...] = total[k * shape[0] : (k + 1) * shape[0]].astype(BF16)

    if ahead:
        work((2, 3), (two, three))
    pl.when(pos[1] == (0 if ahead else 1))(lambda: work((1, 0), (one, own)))


def encode(pos, parts, queries, projected, outs, *results):
    _, _, part, width = parts[0].shape
    tokens = projected[0].shape[0]
    heads = queries[0].shape[1]
    rows = 8 * part
    kv = [pl.BlockSpec((tokens, heads), lambda i: (0, 1)), pl.BlockSpec((tokens, heads), lambda i: (0, 2))]
    args = []
    for wq, proj, wo in zip(queries, projected, outs):
        args += [wq, proj, proj, wo]
    ahead = not results
    n = 5 if ahead else 3
    return pl.pallas_call(
        functools.partial(enc_kernel, ahead),
        grid=(1,),
        in_specs=[SMEM] + [ANY] * 5 + ([VMEM] + kv + [VMEM]) * 2 + [VMEM] * len(results),
        out_specs=[VMEM] * n,
        out_shape=[jax.ShapeDtypeStruct((rows, width), BF16)] * n,
        input_output_aliases={14 + i: i for i in range(len(results))},
        scratch_shapes=[
            pltpu.VMEM((2, 4, 2, part, width), BF16),
            pltpu.VMEM((2 * rows, 2 * heads), BF16),
            pltpu.SemaphoreType.DMA((2, 10)),
        ],
        compiler_params=params(),
        cost_estimate=pl.CostEstimate(
            flops=4 * rows * heads * (4 * width + 4 * GROUP),
            bytes_accessed=8 * rows * width + 8 * heads * width,
            transcendentals=2 * rows * heads,
        ),
        name="encode",
    )(pos, *parts, *args, *results)


def norm_kernel(nz, *refs):
    raw, gain, out = refs[nz:]
    combined = raw[...].astype(F32) + sum(r[...].astype(F32) for r in refs[:nz])
    factor = lax.rsqrt(jnp.mean(combined * combined, axis=-1, keepdims=True) + 1e-06)
    out[...] = (combined * factor * gain[...]).astype(BF16)


def normed(parts, raw, gain):
    return pl.pallas_call(
        functools.partial(norm_kernel, len(parts)),
        in_specs=[VMEM] * (len(parts) + 2),
        out_specs=VMEM,
        out_shape=jax.ShapeDtypeStruct(raw.shape, BF16),
        compiler_params=params(),
        name="normed",
    )(*parts, raw, gain)


def attention(i, core, counts, x, wkvs, queries, out):
    keys, heads = x.shape[0], wkvs[0].shape[1] // 2
    slot = lax.broadcasted_iota(jnp.int32, (GROUP, keys), 1) // (keys // 16) % 2
    first = lax.broadcasted_iota(jnp.int32, (GROUP, 2 * heads), 0) == 0
    allowed = slot < counts[i]
    q = jnp.where(first, queries[i], queries[i + core])
    kvs = [dot(x, wkv[...]).astype(BF16) for wkv in wkvs]
    each_head = [(w, h) for w in range(2) for h in range(0, heads, HEAD_DIM)]
    scores = [
        dot_t(q[:, heads * w + h : heads * w + h + HEAD_DIM], kvs[w][:, h : h + HEAD_DIM]) for w, h in each_head
    ]
    scores = jnp.concatenate(scores, axis=0) * SCALE
    allowed = jnp.concatenate([allowed] * len(each_head), axis=0)
    scores = jnp.where(allowed, scores, -1e30)
    raised = jnp.exp(scores - jnp.max(scores, axis=-1, keepdims=True))
    share = (raised / jnp.sum(raised, axis=-1, keepdims=True)).astype(BF16)
    for k, (w, h) in enumerate(each_head):
        value = kvs[w][:, heads + h : heads + h + HEAD_DIM]
        out[:, pl.ds(heads * w + h, HEAD_DIM)] = dot(share[k * GROUP : (k + 1) * GROUP], value).astype(BF16)


def attend_kernel(pos, counts, rows, own_kv, other_kv, queries, out):
    attention(pos[0], pos[1], counts, rows[...], (own_kv, other_kv), queries, out)


def attend_more_kernel(pos, counts, one, two, own_kv, other_kv, queries, first, out, pick):
    out[0] = first[...]
    for flip, x in (1, one), (2, two):
        attention(pos[0] ^ flip, pos[1], counts, x[...], (own_kv, other_kv), queries, out.at[flip])
    z = pos[0]
    pick[...] = jnp.where(z == 3, out[0], jnp.where(z == 2, out[1], out[2]))


def attend(pos, counts, rows, wkvs, queries, *earlier):
    keys, width = rows[0].shape
    both = wkvs[0].shape[1]
    n = len(rows)
    single = jax.ShapeDtypeStruct((GROUP, both), BF16)
    return pl.pallas_call(
        attend_more_kernel if earlier else attend_kernel,
        in_specs=[SMEM, SMEM] + [VMEM] * (n + 3 + len(earlier)),
        out_specs=[VMEM, VMEM] if earlier else VMEM,
        out_shape=[jax.ShapeDtypeStruct((3, GROUP, both), BF16), single] if earlier else single,
        compiler_params=params(),
        cost_estimate=pl.CostEstimate(
            flops=4 * n * keys * both * (width + GROUP),
            bytes_accessed=2 * (2 * width * both + n * keys * width),
            transcendentals=n * GROUP * keys * both // HEAD_DIM,
        ),
        name="attend",
    )(pos, counts, *rows, *wkvs, queries, *earlier)


def loads_of(wos, loaded, sems):
    heads, model = wos[0].shape
    pieces = sems.shape[1]
    piece = model // pieces
    return [
        [
            pltpu.make_async_copy(
                wos[w].at[:, pl.ds(p * piece, piece)], loaded.at[p, pl.ds(w * heads, heads)], sems.at[w, p]
            )
            for w in range(2)
        ]
        for p in range(pieces)
    ]


def last_kernel(pos, counts, middle, far, own_kv, other_kv, queries, *refs):
    atts, before, wos, outs, (got, held, loaded, sems) = refs[0], refs[1], refs[2:4], refs[4:8], refs[8:]
    loads = loads_of(wos, loaded, sems)
    for load in sum(loads, []):
        load.start()
    z, core = pos[0], pos[1]
    x = jnp.where((z == 1) | (z == 2), middle[...], far[...])
    attention(z ^ 3, core, counts, x, (own_kv, other_kv), queries, got)
    held[0] = before[...]
    for flip in range(4):
        held[(z ^ flip) + 1] = got[...] if flip == 3 else atts[flip]
    first = lax.broadcasted_iota(jnp.int32, got.shape, 0) == 0
    rows = []
    for flip in range(4):
        i = (z ^ flip) + 1
        rows.append(jnp.where(first, held[i], held[i - core]))
    rows = jnp.concatenate(rows, axis=0)
    piece = loaded.shape[2]
    for p, pair in enumerate(loads):
        for load in pair:
            load.wait()
        result = dot(rows, loaded[p]).astype(BF16)
        for flip in range(4):
            outs[flip][:, pl.ds(p * piece, piece)] = result[flip * GROUP : (flip + 1) * GROUP]


def last_attend(pos, counts, middle, far, wkvs, queries, atts, before, wos):
    keys, width = middle.shape
    heads, model = wos[0].shape
    pieces = 4
    return pl.pallas_call(
        last_kernel,
        in_specs=[SMEM, SMEM] + [VMEM] * 7 + [HBM, ANY],
        out_specs=[VMEM] * 5,
        out_shape=[jax.ShapeDtypeStruct((GROUP, model), BF16)] * 4 + [jax.ShapeDtypeStruct(before.shape, BF16)],
        scratch_shapes=[
            pltpu.VMEM((5,) + before.shape, BF16),
            pltpu.VMEM((pieces, 2 * heads, model // pieces), BF16),
            pltpu.SemaphoreType.DMA((2, pieces)),
        ],
        compiler_params=params(),
        cost_estimate=pl.CostEstimate(
            flops=16 * GROUP * heads * model + 8 * keys * heads * (width + GROUP),
            bytes_accessed=4 * heads * model + 8 * GROUP * model,
            transcendentals=2 * GROUP * keys * heads // HEAD_DIM,
        ),
        name="last_attend",
    )(pos, counts, middle, far, *wkvs, queries, atts, before, *wos)


def late_kernel(before, own_w, other_w, out, loaded, sems):
    loads = loads_of((own_w, other_w), loaded, sems)
    for load in sum(loads, []):
        load.start()
    first = lax.broadcasted_iota(jnp.int32, before.shape, 0) == 0
    rows = jnp.where(first, 0.0, before[...].astype(F32)).astype(BF16)
    piece = loaded.shape[2]
    for p, pair in enumerate(loads):
        for load in pair:
            load.wait()
        out[:, pl.ds(p * piece, piece)] = dot(rows, loaded[p]).astype(BF16)


def late_out(before, wos):
    heads, model = wos[0].shape
    pieces = 4
    return pl.pallas_call(
        late_kernel,
        in_specs=[VMEM, HBM, ANY],
        out_specs=VMEM,
        out_shape=jax.ShapeDtypeStruct((GROUP, model), BF16),
        scratch_shapes=[
            pltpu.VMEM((pieces, 2 * heads, model // pieces), BF16),
            pltpu.SemaphoreType.DMA((2, pieces)),
        ],
        compiler_params=params(),
        cost_estimate=pl.CostEstimate(
            flops=4 * GROUP * heads * model, bytes_accessed=4 * heads * model, transcendentals=0
        ),
        name="late_out",
    )(before, *wos)


def by_groups(
    tokens,
    nbr_embed,
    neighbour_table,
    valid_counts,
    dec_proj,
    enc_query,
    enc_out,
    enc_gain,
    nbr_proj,
    out_proj,
):
    nz = lax.axis_size("nbr") // 2
    n_seq = lax.axis_size("seq")
    seq_index = lax.axis_index("seq")
    member = lax.axis_index("nbr")
    z, core = member // 2, member % 2
    pos = jnp.stack([z, core]).astype(jnp.int32)
    width = dec_proj.shape[2]
    ch_grp, slots = neighbour_table.shape
    nb_grp, share, enc_width = nbr_embed.shape

    ids = neighbour_table.reshape(nz, 2, slots) - seq_index * nb_grp

    def picked(c):
        mine = lax.dynamic_index_in_dim(ids, c, 1, False).reshape(-1)
        return jnp.take(nbr_embed, mine, axis=0, mode="clip").reshape(nz, slots * share, enc_width)

    held = lax.optimization_barrier

    two, one = hop(tokens, 2), hop(tokens, 1)
    nbr_own = jnp.stack([picked(core), swapped(picked(1 - core), nz)])
    two, one, own, nbr_own, enc_query, enc_out, nbr_proj, out_proj = held(
        (two, one, tokens, nbr_own, enc_query, enc_out, nbr_proj, out_proj)
    )
    far, middle = hop(two, 1, MIDDLE), hop(own, 3, MIDDLE)
    wkv = nbr_proj.reshape(enc_width, 2 * width)
    encos, wkvs, outps = [(w, swapped(w, nz)) for w in (enc_out, wkv, out_proj)]
    column = jnp.stack([own, one, two, jnp.where((z == 1) | (z == 2), middle, far)])
    column, encos, wkvs, outps = held((column, encos, wkvs, outps))
    other = swapped(column, nz)
    encqs = (enc_query, swapped(enc_query, nz))
    nbr_two, nbr_one = hop(nbr_own, 2), hop(nbr_own, 1)
    mine, theirs = project(pos, column, other, dec_proj.transpose(1, 0, 2))
    mine, theirs, nbr_two, nbr_one, nbr_own, encqs = held((mine, theirs, nbr_two, nbr_one, nbr_own, encqs))
    nbrs = (nbr_own, nbr_one, nbr_two, hop(nbr_own, 3, MIDDLE), hop(nbr_two, 1, MIDDLE))
    projected = [p.reshape(nz * GROUP, 3 * width) for p in (mine, swapped(theirs, nz))]

    last = jnp.concatenate([p[:, :width].reshape(nz, GROUP, width)[:, GROUP - 1 :] for p in projected], axis=2)
    others = jnp.concatenate([theirs[:, :, :width], swapped(mine[:, :, :width], nz)], axis=2)
    counts = lax.dynamic_index_in_dim(
        lax.dynamic_slice_in_dim(valid_counts, seq_index * ch_grp, ch_grp, 0).reshape(nz, 2), core, 1, False
    )

    nbrs, others, last = held((nbrs, others, last))
    queries = jnp.concatenate([last, others[:, : GROUP - 1]], axis=1)
    odd = range(1, 2 * nz, 2)
    back = [((q + 1) * 2 * nz + n, q * 2 * nz + n) for q in range(n_seq - 1) for n in odd]
    queries = jnp.concatenate([queries, lax.ppermute(queries[:1], ("seq", "nbr"), back)])
    two, three, *rest = encode(pos, nbrs, encqs, projected, encos)
    raws = []

    def part(flips):
        if flips == (2, 3):
            return two, three
        one, own, raw = encode(pos, nbrs, encqs, projected, encos, *rest)
        raws.append(raw)
        return one, own

    arrived = scattered(part)
    enc_own = normed(arrived, raws[0], enc_gain.reshape(1, -1))
    enc_two, enc_one = hop(enc_own, 2), hop(enc_own, 1)
    first = attend(pos, counts, (enc_own,), wkvs, queries)
    enc_two, enc_mine, first = held((enc_two, enc_own, first))
    enc_middle, enc_far = hop(enc_mine, 3, MIDDLE), hop(enc_two, 1, MIDDLE)
    atts, pick = attend(pos, counts, (enc_one, enc_two), wkvs, queries, first)

    def onward(x, chips):
        route = [(q * 2 * nz + 2 * i + 1, (q + 1) * 2 * nz + 2 * i + 1) for q in range(n_seq - 1) for i in chips]
        got = lax.ppermute(x, ("seq", "nbr"), route)
        return jnp.where((seq_index * ch_grp * GROUP) % SEQ_LEN == 0, 0, got).astype(BF16)

    before = onward(pick, (1, 2, 3))
    *outs, last = last_attend(pos, counts, enc_middle, enc_far, wkvs, queries, atts, before, outps)
    arrived = scattered(lambda flips: [outs[flip] for flip in flips])
    arrived.append(late_out(onward(last, (0,)), outps))
    mine = sum(part.astype(F32) for part in arrived).astype(BF16)
    theirs = swapped(mine, nz)
    cross_out = jnp.concatenate([theirs[1:], mine[:1]], axis=0)

    encoded = enc_own.reshape(nz, 2, slots, share, enc_width)
    encoded = jnp.where(core == 0, encoded, encoded[:, ::-1]).transpose(2, 0, 1, 3, 4).reshape(-1, enc_width)
    return (cross_out, encoded)


def local(*args):
    tokens, table = args[0], args[2]
    chips = lax.axis_size("nbr") // 2
    if chips == 4 and table.shape[0] == 8 and tokens.shape[0] == GROUP:
        return by_groups(*args)
    return by_heads(*args)


def solution(mesh):
    return jax.shard_map(
        local,
        mesh=mesh,
        in_specs=(
            P(("seq", "nbr"), None),
            P("seq", "nbr", None),
            P("seq", None),
            P(),
            P(None, None, "nbr"),
            P(None, "nbr"),
            P("nbr", None),
            P(),
            P(None, None, "nbr"),
            P("nbr", None),
        ),
        out_specs=(P(("seq", "nbr"), None), P(("seq", "nbr"), None)),
        check_vma=False,
    )
```
